512 devices in a mesh: cp: 64 (over z_lo, y, core), tp: 8 (over z_hi, x).
Axes of the slice: x: 4, y: 8, z: 8 (z_hi: 2, z_lo: 4; z = z_hi * 4 + z_lo), core: 2. Of those that a mesh axis runs over, the one named last changes fastest.
Arguments:
- queries: bfloat16 [8192, 8192], P('cp', 'tp'), may hold values from -8 to 8
- keys: bfloat16 [8192, 1024], P('cp', 'tp'), may hold values from -8 to 8
- values: bfloat16 [8192, 1024], P('cp', 'tp'), may hold values from -6 to 6
- positions: int32 [8192], replicated, may hold values from 0 to 8191, as said below
- counts: int32 [64], replicated, may hold values from 1 to 128, as said below
- owner_row: int32 [8, 64], replicated, may hold values from 0 to 63, as said below
- owner_col: int32 [8, 64], replicated, may hold values from 0 to 7, as said below
- owner_slot: int32 [8, 64], replicated, may hold values from 0 to 1
Outputs:
- attended: bfloat16 [8192, 8192], P('cp', 'tp')
- pool_keys: bfloat16 [1024, 128, 128], P(('cp', 'tp'))
- pool_values: bfloat16 [1024, 128, 128], P(('cp', 'tp'))
The draws below stay inside these ranges and needn't reach their ends.
Inputs may be any that keep to these rules, and one draw needn't show every extreme that they name: A permutation of the positions. The rows of index c of cp are two runs of 64 consecutive positions, each starting at a multiple of 64: run j first, then run 2 * 64 - 1 - j, every j from 0 to 64 - 1 once. `counts`: some page holds 128 valid tokens and some page holds one. `owner_row`: for every kv head, every index of cp owns exactly one page. `owner_col`: no two (kv head, page) pairs name the same owner row, column and slot; a device keeps at most 2 pages and some device keeps exactly 2.
All inputs are finite; a program needn't handle non-finite values.
Results may differ from the reference program's by a relative error of at most 0.012.
The reference program's roundings to bfloat16 on the way count: a program that leaves them out, or rounds other values in their place, can miss the bound.
Values may be sent and summed in bfloat16 or wider, within the bound.
No kernel may reach another device: no remote copies, remote signals or barrier semaphores. Data moves between devices by JAX's collectives and lax.ppermute only.
A program may use at most 64 MiB of HBM per device.

```python
import math
import jax
import jax.numpy as jnp
from jax import lax

QH = 64
KVH = 8
HD = 128
PAGE = 128
TOK_DEV = 128
TOKENS = 8192
HALF = 64
PAGES = 64
SLOTS = 2
N_CP = 64
N_TP = 8


def owner_tables(key):
    per_row = TOK_DEV // PAGE
    span = N_TP * SLOTS
    first_key, second_key, third_key = jax.random.split(key, 3)
    orders = jax.vmap(lambda sub_key: jax.random.permutation(sub_key, PAGES))(jax.random.split(first_key, KVH)).astype(jnp.int32)
    row_ids = orders // per_row
    entries = jnp.arange(KVH, dtype=jnp.int32)[:, None] * per_row + orders % per_row
    col_orders = jax.vmap(lambda sub_key: jax.random.permutation(sub_key, N_TP))(jax.random.split(second_key, N_CP)).astype(jnp.int32)
    later_slots = jax.vmap(lambda sub_key: jax.random.permutation(sub_key, span - SLOTS))(jax.random.split(third_key, N_CP)).astype(jnp.int32)
    later = later_slots[row_ids, jnp.clip(entries - SLOTS, 0, span - SLOTS - 1)]
    placed = jnp.where(entries < SLOTS, entries, SLOTS + later)
    columns = col_orders[row_ids, placed // SLOTS]
    slot_ids = placed % SLOTS
    return (row_ids.astype(jnp.int32), columns.astype(jnp.int32), slot_ids.astype(jnp.int32))


def draw_owner_row(key, part):
    tables = owner_tables(key)
    return tables[0]


def draw_owner_col(key, part):
    tables = owner_tables(key)
    return tables[1]


def draw_owner_slot(key, part):
    tables = owner_tables(key)
    return tables[2]


def draw_positions(key, part):
    key = jax.random.fold_in(key, 1)
    orders = jax.random.permutation(key, N_CP).astype(jnp.int32)
    runs = jnp.stack([orders, 2 * N_CP - 1 - orders], axis=1).reshape(-1)
    offsets = jnp.arange(HALF, dtype=jnp.int32)
    return (runs[:, None] * HALF + offsets[None, :]).reshape(-1).astype(jnp.int32)


def draw_counts(key, part):
    key = jax.random.fold_in(key, 2)
    first_key, second_key, third_key = jax.random.split(key, 3)
    drawn = jax.random.randint(first_key, (PAGES,), 1, PAGE + 1).astype(jnp.int32)
    full_at = jax.random.randint(second_key, (), 0, PAGES)
    short_at = (full_at + 1 + jax.random.randint(third_key, (), 0, PAGES - 1)) % PAGES
    return drawn.at[full_at].set(PAGE).at[short_at].set(1).astype(jnp.int32)


def draw_queries(key, part):
    base_key = key
    key = jax.random.fold_in(base_key, 5)
    return jnp.clip(jax.random.normal(key, (TOKENS, QH * HD)), -5.0, 5.0).astype(jnp.bfloat16)


def draw_keys(key, part):
    base_key = key
    key = jax.random.fold_in(base_key, 6)
    return jnp.clip(jax.random.normal(key, (TOKENS, KVH * HD)), -5.0, 5.0).astype(jnp.bfloat16)


def level_of(own_key, dims, cuts, low, top_value):
    gain = 1.0
    for position, parts in cuts:
        heights = jax.random.uniform(jax.random.fold_in(jax.random.fold_in(own_key, 6), position), (parts,), jnp.float32, low / len(cuts), top_value / len(cuts))
        gain = gain * jnp.repeat(jnp.exp(heights), dims[position] // parts).reshape((-1,) + (1,) * (len(dims) - 1 - position))
    return gain


def gaussian(stream_key, dims, scale, limit, cuts=(), held_as=jnp.bfloat16):
    factor_of = level_of(stream_key, dims, cuts, -0.22, 0.18) if cuts else 1.0
    result = jax.random.normal(stream_key, dims, jnp.float32) * scale * factor_of
    return jnp.minimum(jnp.maximum(result, -limit), limit).astype(held_as)


def setup_inputs(seed: int = 0) -> dict:
    key_of = jax.random.split(jax.random.key(seed), 9)
    queries = draw_queries(jax.random.fold_in(key_of[8], 71), 0)
    keys = draw_keys(jax.random.fold_in(key_of[8], 71), 0)
    values = gaussian(key_of[2], (TOKENS, KVH * HD), 1.0, 6.0, ((0, 64), (1, 8)))
    positions = draw_positions(jax.random.fold_in(key_of[8], 71), 0)
    counts = draw_counts(jax.random.fold_in(key_of[8], 71), 0)
    owner_row = draw_owner_row(jax.random.fold_in(key_of[8], 71), 0)
    owner_col = draw_owner_col(jax.random.fold_in(key_of[8], 71), 0)
    owner_slot = draw_owner_slot(jax.random.fold_in(key_of[8], 71), 0)
    return {"queries": queries, "keys": keys, "values": values, "positions": positions, "counts": counts, "owner_row": owner_row, "owner_col": owner_col, "owner_slot": owner_slot}


theta_base = 500000.0
neg_big = -1e+30

def rotate(tensor, token_pos):
    half_dim = tensor.shape[-1] // 2
    inv_freq = theta_base ** (-(jnp.arange(half_dim, dtype=jnp.float32) * 2.0 / tensor.shape[-1]))
    angles = token_pos.astype(jnp.float32)[:, None] * inv_freq[None, :]
    cos_part = jnp.concatenate([jnp.cos(angles), jnp.cos(angles)], axis=-1)[:, None, :]
    sin_part = jnp.concatenate([jnp.sin(angles), jnp.sin(angles)], axis=-1)[:, None, :]
    turned = jnp.concatenate([-tensor[..., half_dim:], tensor[..., :half_dim]], axis=-1)
    return tensor * cos_part + turned * sin_part

def reference(queries, keys, values, positions, counts, owner_row, owner_col, owner_slot):
    group = QH // KVH
    score_scale = 1.0 / math.sqrt(HD)
    q_rot = rotate(queries.astype(jnp.float32).reshape(TOKENS, QH, HD), positions).astype(jnp.bfloat16)
    k_rot = rotate(keys.astype(jnp.float32).reshape(TOKENS, KVH, HD), positions).astype(jnp.bfloat16)
    key_ok = positions % PAGE < counts[positions // PAGE]
    q_float = lax.optimization_barrier(q_rot).astype(jnp.float32).reshape(TOKENS, KVH, group, HD)
    k_float = lax.optimization_barrier(k_rot).astype(jnp.float32)
    v_heads = values.reshape(TOKENS, KVH, HD)
    v_float = v_heads.astype(jnp.float32)
    block_rows = math.gcd(TOK_DEV, 128)

    def one_block(first_row):
        q_block = lax.dynamic_slice_in_dim(q_float, first_row, block_rows, 0)
        q_pos = lax.dynamic_slice_in_dim(positions, first_row, block_rows, 0)
        scores = jnp.einsum('tkgd,nkd->kgtn', q_block, k_float) * score_scale
        allowed = (positions[None, :] <= q_pos[:, None]) & key_ok[None, :]
        scores = jnp.where(allowed, scores, neg_big)
        row_top = lax.optimization_barrier(jnp.max(scores, axis=-1, keepdims=True))
        weights = jnp.where(allowed, jnp.exp(scores - row_top), 0.0)
        totals = lax.optimization_barrier(jnp.sum(weights, axis=-1))
        rounded = lax.optimization_barrier(weights.astype(jnp.bfloat16)).astype(jnp.float32)
        summed = jnp.einsum('kgtn,nkd->tkgd', rounded, v_float)
        return (summed / totals.transpose(2, 0, 1)[..., None]).astype(jnp.bfloat16)
    starts = jnp.arange(TOKENS // block_rows, dtype=jnp.int32) * block_rows
    attended = lax.map(one_block, starts).reshape(TOKENS, QH * HD)
    inverse = jnp.zeros((TOKENS,), jnp.int32).at[positions].set(jnp.arange(TOKENS, dtype=jnp.int32))
    ok_seq = key_ok[inverse][:, None, None]
    zero_half = jnp.zeros((), jnp.bfloat16)
    k_seq = jnp.where(ok_seq, k_rot[inverse], zero_half)
    v_seq = jnp.where(ok_seq, v_heads[inverse], zero_half)
    k_pages = k_seq.reshape(PAGES, PAGE, KVH, HD).transpose(2, 0, 1, 3).reshape(KVH * PAGES, PAGE, HD)
    v_pages = v_seq.reshape(PAGES, PAGE, KVH, HD).transpose(2, 0, 1, 3).reshape(KVH * PAGES, PAGE, HD)
    flat_slot = ((owner_row * N_TP + owner_col) * SLOTS + owner_slot).reshape(-1).astype(jnp.int32)
    pool_keys = jnp.zeros((N_CP * N_TP * SLOTS, PAGE, HD), jnp.bfloat16).at[flat_slot].set(k_pages)
    pool_values = jnp.zeros((N_CP * N_TP * SLOTS, PAGE, HD), jnp.bfloat16).at[flat_slot].set(v_pages)
    return (attended, pool_keys, pool_values)
```

```python
import functools
import math

import jax
import jax.numpy as jnp
import numpy as np
from jax import lax
from jax.experimental import pallas as pl
from jax.experimental.pallas import tpu as pltpu
from jax.sharding import PartitionSpec as P

KVH = 8
HD = 128
PAGE = 128
HALF = 64
ROWS = 128
N_CP = 64
N_Z = 4
N_Y = 8
N_TP = 8
N_X = 4
SRC = N_CP // 2
CHUNK = 4
RUNS = 2 * N_CP
BIG = 1e30

THETA = 500000.0
FREQ = np.concatenate([THETA ** (-np.arange(HALF) * 2.0 / HD)] * 2).astype(np.float32)[None, :]
OFFSETS = (0, -1, 1, -2, 2, -3, 3, 4)


def cp_index(z, y, core):
    return ((z % N_Z) * N_Y + y % N_Y) * 2 + core


def cp_pairs(step):
    return [
        (cp_index(z, y, c), cp_index(z, y + step, c))
        for z in range(N_Z)
        for y in range(N_Y)
        for c in range(2)
    ]


CORE_PAIRS = [(i, i ^ 1) for i in range(N_CP)]
Z_GROUPS = [[cp_index(z, y, c) for z in range(N_Z)] for y in range(N_Y) for c in range(2)]
ZHI_PAIRS = [(i, (i + N_X) % N_TP) for i in range(N_TP)]


def x_pairs(step):
    return [(i, (i // N_X) * N_X + (i + step) % N_X) for i in range(N_TP)]


def angles_of(freq, first_run, second_run, rows):
    row = lax.broadcasted_iota(jnp.int32, (rows, HD), 0)
    pos = jnp.where(row < HALF, first_run * HALF + row, second_run * HALF + row - HALF)
    angles = pos.astype(jnp.float32) * freq
    low = lax.broadcasted_iota(jnp.int32, (rows, HD), 1) < HALF
    sin = jnp.sin(angles)
    return jnp.cos(angles), jnp.where(low, -sin, sin)


def turned(x, cos, sin):
    return x * cos + pltpu.roll(x, HALF, 1) * sin


def pack_kernel(runs, keys, values, freq, out):
    first = runs[0]
    cos, sin = angles_of(freq[...], first, RUNS - 1 - first, ROWS)
    k_rot = turned(keys[...].astype(jnp.float32), cos, sin).astype(jnp.bfloat16)
    v = values[...]
    for i in range(N_Z):
        out[i, 0] = k_rot
        out[i, 1] = v


def pack(my_run, keys, values):
    smem = pl.BlockSpec(memory_space=pltpu.SMEM)
    vmem = pl.BlockSpec(memory_space=pltpu.VMEM)
    return pl.pallas_call(
        pack_kernel,
        out_shape=jax.ShapeDtypeStruct((N_Z, 2, ROWS, HD), jnp.bfloat16),
        in_specs=[smem, vmem, vmem, vmem],
        out_specs=vmem,
        cost_estimate=pl.CostEstimate(flops=1_000_000, bytes_accessed=400_000, transcendentals=0),
        name="pack",
    )(my_run, keys, values, jnp.asarray(FREQ))


def attend_kernel(place, run_of, counts, queries, freq, own, other, out, kv, q_rot, blk, sems):
    copies = [
        pltpu.make_async_copy(own, kv.at[pl.ds(0, SRC)], sems.at[0]),
        pltpu.make_async_copy(other, kv.at[pl.ds(SRC, SRC)], sems.at[1]),
    ]
    for copy in copies:
        copy.start()
    y, core = place[0], place[1]
    me = place[2]
    my_run = run_of[me]

    for side in range(2):
        for i, off in enumerate(OFFSETS):
            src_y = lax.rem(y + off + N_Y, N_Y)
            src_c = core if side == 0 else 1 - core
            for z in range(N_Z):
                blk[run_of[(z * N_Y + src_y) * 2 + src_c]] = side * SRC + i * N_Z + z

    cos, sin = angles_of(freq[...], my_run, RUNS - 1 - my_run, ROWS)
    for h in range(KVH):
        x = turned(queries[:, h * HD : (h + 1) * HD].astype(jnp.float32), cos, sin)
        x = x.astype(jnp.bfloat16)
        q_rot[0, h * HALF : (h + 1) * HALF, :] = x[:HALF]
        q_rot[1, h * HALF : (h + 1) * HALF, :] = x[HALF:]
    for copy in copies:
        copy.wait()

    cols = KVH * HALF
    width = CHUNK * HALF
    scale = math.log2(math.e) / math.sqrt(HD)
    key_at = lax.broadcasted_iota(jnp.int32, (HALF, HD), 0)
    dot = functools.partial(lax.dot_general, preferred_element_type=jnp.float32)

    def half_block(run):
        second = run >= N_CP
        j = jnp.where(second, RUNS - 1 - run, run)
        b = blk[jnp.clip(j, 0, N_CP - 1)]
        rows = pl.ds(pl.multiple_of(jnp.where(second, HALF, 0), HALF), HALF)
        valid = jnp.clip(counts[lax.shift_right_logical(run, 1)] - (run & 1) * HALF, 0, HALF)
        return kv[b, 0, rows, :], kv[b, 1, rows, :], valid

    def step(q, q_run, last, i, state):
        top, total, acc = state
        ks, vs, biases = [], [], []
        for r in range(CHUNK):
            run = i * CHUNK + r
            k, v, valid = half_block(jnp.minimum(run, RUNS - 1))
            ks.append(k)
            vs.append(v)
            if last:
                valid = jnp.where(run <= q_run, valid, 0)
            biases.append(jnp.where(key_at < valid, 0.0, -BIG))
        keys = jnp.concatenate(ks, axis=0)
        vals = jnp.concatenate(vs, axis=0)
        bias = jnp.concatenate(biases, axis=0)
        s = dot(keys, q, (((1,), (1,)), ((), ()))) * scale
        s = s + jnp.concatenate([bias] * (cols // HD), axis=1)
        if last:
            key = lax.broadcasted_iota(jnp.int32, (width, cols), 0)
            row = lax.broadcasted_iota(jnp.int32, (width, cols), 1)
            ahead = (q_run - i * CHUNK) * HALF
            s = jnp.where(key <= ahead + (row & (HALF - 1)), s, -BIG)
        new_top = jnp.maximum(top, jnp.max(s, axis=0, keepdims=True))
        factor = jnp.exp2(top - new_top)
        w = jnp.exp2(s - new_top)
        total = total * factor + jnp.sum(w, axis=0, keepdims=True)
        acc = acc * factor + dot(vals, w.astype(jnp.bfloat16), (((0,), (0,)), ((), ())))
        return new_top, total, acc

    for part in range(2):
        q = q_rot[part]
        q_run = my_run if part == 0 else RUNS - 1 - my_run
        state = (
            jnp.full((1, cols), -BIG, jnp.float32),
            jnp.zeros((1, cols), jnp.float32),
            jnp.zeros((HD, cols), jnp.float32),
        )
        full = lax.shift_right_logical(q_run, CHUNK.bit_length() - 1)
        state = lax.fori_loop(0, full, functools.partial(step, q, q_run, False), state)
        _, total, acc = step(q, q_run, True, full, state)
        res = jnp.transpose(acc / total).astype(jnp.bfloat16)
        for h in range(KVH):
            out[part * HALF : (part + 1) * HALF, h * HD : (h + 1) * HD] = res[
                h * HALF : (h + 1) * HALF
            ]


def attend(place, run_of, counts, queries, own, other):
    smem = pl.BlockSpec(memory_space=pltpu.SMEM)
    vmem = pl.BlockSpec(memory_space=pltpu.VMEM)
    anywhere = pl.BlockSpec(memory_space=pl.ANY)
    return pl.pallas_call(
        attend_kernel,
        out_shape=jax.ShapeDtypeStruct((ROWS, KVH * HD), jnp.bfloat16),
        in_specs=[smem, smem, smem, vmem, vmem, anywhere, anywhere],
        out_specs=vmem,
        scratch_shapes=[
            pltpu.VMEM((2 * SRC, 2, ROWS, HD), jnp.bfloat16),
            pltpu.VMEM((2, KVH * HALF, HD), jnp.bfloat16),
            pltpu.SMEM((N_CP,), jnp.int32),
            pltpu.SemaphoreType.DMA((2,)),
        ],
        compiler_params=pltpu.CompilerParams(vmem_limit_bytes=40 * 2**20),
        cost_estimate=pl.CostEstimate(
            flops=20_000_000_000, bytes_accessed=5_000_000, transcendentals=4_000_000
        ),
        name="attend",
    )(place, run_of, counts, queries, jnp.asarray(FREQ), own, other)


def pick_kernel(where, own_a, other_a, own_b, other_b, out):
    row = lax.broadcasted_iota(jnp.int32, (HALF, HD), 0)
    for half, own, other in ((0, own_a, other_a), (1, own_b, other_b)):
        mine = where[half * 4] == 1
        keep = row < where[half * 4 + 3]
        for i in range(2):
            block = jnp.where(mine, own[0, i], other[0, i])
            out[i, half * HALF : (half + 1) * HALF, :] = jnp.where(
                keep, block, jnp.zeros_like(block)
            )


def pick(where, own, other):
    def spec(half):
        return pl.BlockSpec((1, 2, HALF, HD), lambda i, w: (w[half * 4 + 1], 0, w[half * 4 + 2], 0))

    return pl.pallas_call(
        pick_kernel,
        grid_spec=pltpu.PrefetchScalarGridSpec(
            num_scalar_prefetch=1,
            grid=(1,),
            in_specs=[spec(0), spec(0), spec(1), spec(1)],
            out_specs=pl.BlockSpec((2, PAGE, HD), lambda i, w: (0, 0, 0)),
        ),
        out_shape=jax.ShapeDtypeStruct((2, PAGE, HD), jnp.bfloat16),
        cost_estimate=pl.CostEstimate(flops=100_000, bytes_accessed=200_000, transcendentals=0),
        name="pick",
    )(where, own, other, own, other)


def place_kernel(table, near, right, left, far, pool_k, pool_v):
    zero = jnp.zeros((PAGE, HD), jnp.bfloat16)
    for slot in range(2):
        pool_k[slot] = zero
        pool_v[slot] = zero
    for i, pages in enumerate((near, right, left, far)):
        for hi in range(2):
            for slot in range(2):

                @pl.when(table[i * 2 + hi] == slot)
                def _(pages=pages, hi=hi, slot=slot):
                    pool_k[slot] = pages[hi, 0]
                    pool_v[slot] = pages[hi, 1]


def place(table, near, right, left, far):
    smem = pl.BlockSpec(memory_space=pltpu.SMEM)
    vmem = pl.BlockSpec(memory_space=pltpu.VMEM)
    shape = jax.ShapeDtypeStruct((2, PAGE, HD), jnp.bfloat16)
    return pl.pallas_call(
        place_kernel,
        out_shape=(shape, shape),
        in_specs=[smem, vmem, vmem, vmem, vmem],
        out_specs=(vmem, vmem),
        cost_estimate=pl.CostEstimate(flops=100_000, bytes_accessed=800_000, transcendentals=0),
        name="place",
    )(table, near, right, left, far)


def shards(queries, keys, values, positions, counts, owner_row, owner_col, owner_slot):
    cp_rank = lax.axis_index("cp")
    tp_rank = lax.axis_index("tp")
    y = (cp_rank // 2) % N_Y
    core = cp_rank % 2
    run_of = positions.reshape(N_CP, ROWS)[:, 0] // HALF
    my_run = lax.dynamic_slice_in_dim(run_of, cp_rank, 1, 0)

    packed = pack(my_run, keys, values)
    unit = lax.all_to_all(packed, "cp", 0, 0, axis_index_groups=Z_GROUPS)
    ahead, back = cp_pairs(1), cp_pairs(-1)
    f1 = lax.ppermute(unit, "cp", ahead)
    b1 = lax.ppermute(unit, "cp", back)
    f2 = lax.ppermute(f1, "cp", ahead)
    b2 = lax.ppermute(b1, "cp", back)
    f3 = lax.ppermute(f2, "cp", ahead)
    b3 = lax.ppermute(b2, "cp", back)
    f4 = lax.ppermute(f3, "cp", ahead)
    own = jnp.concatenate([unit, f1, b1, f2, b2, f3, b3, f4], axis=0)
    other = lax.ppermute(own, "cp", CORE_PAIRS)

    here = owner_row == cp_rank
    pages = jnp.sum(jnp.where(here, jnp.arange(N_CP, dtype=jnp.int32)[None, :], 0), axis=1)
    cols = jnp.sum(jnp.where(here, owner_col, 0), axis=1)
    slots = jnp.sum(jnp.where(here, owner_slot, 0), axis=1)
    page = lax.dynamic_slice_in_dim(pages, tp_rank, 1, 0)
    valid = jnp.sum(jnp.where(jnp.arange(N_CP) == page, counts, 0))
    where = []
    for half in range(2):
        run = page[0] * 2 + half
        second = run >= N_CP
        j = jnp.where(second, RUNS - 1 - run, run)
        src = jnp.sum(jnp.where(run_of == j, jnp.arange(N_CP, dtype=jnp.int32), 0))
        src_y = (src // 2) % N_Y
        off = (src_y - y) % N_Y
        order = jnp.where(off <= N_Y // 2, 2 * off, 2 * (N_Y - off) - 1)
        order = jnp.where(off == N_Y // 2, N_Y - 1, order)
        where += [
            (src % 2 == core).astype(jnp.int32),
            order * N_Z + src // (2 * N_Y),
            second.astype(jnp.int32),
            jnp.clip(valid - half * HALF, 0, HALF),
        ]
    picked = pick(jnp.stack(where), own, other)

    across = lax.ppermute(picked, "tp", ZHI_PAIRS)
    near = jnp.stack([picked, across])
    right = lax.ppermute(near, "tp", x_pairs(1))
    left = lax.ppermute(near, "tp", x_pairs(-1))
    far = lax.ppermute(near, "tp", x_pairs(2))

    attended = attend(jnp.stack([y, core, cp_rank]), run_of, counts, queries, own, other)

    goes = jnp.where(cols == tp_rank, slots, -1)
    hi, x = tp_rank // N_X, tp_rank % N_X
    heads = jnp.stack(
        [((hi + d) % 2) * N_X + (x - step) % N_X for step in (0, 1, -1, 2) for d in range(2)]
    )
    matches = heads[:, None] == jnp.arange(KVH)[None, :]
    table = jnp.sum(jnp.where(matches, goes[None, :], 0), axis=1)
    pool_keys, pool_values = place(table, near, right, left, far)
    return attended, pool_keys, pool_values


def solution(mesh):
    return jax.shard_map(
        shards,
        mesh=mesh,
        in_specs=(P("cp", "tp"), P("cp", "tp"), P("cp", "tp"), P(), P(), P(), P(), P()),
        out_specs=(P("cp", "tp"), P(("cp", "tp"), None, None), P(("cp", "tp"), None, None)),
        check_vma=False,
    )
```

```python
import functools
import math

import jax
import jax.numpy as jnp
import numpy as np
from jax import lax
from jax.experimental import pallas as pl
from jax.experimental.pallas import tpu as pltpu
from jax.sharding import PartitionSpec as P

KVH = 8
HD = 128
PAGE = 128
HALF = 64
ROWS = 128
N_CP = 64
N_Z = 4
N_Y = 8
N_TP = 8
N_X = 4
SRC = N_CP // 2
FIRST = 28
REST = N_CP - FIRST
LANES = 128
RUNS = 2 * N_CP
BIG = 1e30

THETA = 500000.0
FREQ = np.concatenate([THETA ** (-np.arange(HALF) * 2.0 / HD)] * 2).astype(np.float32)[None, :]
OFFSETS = (0, -1, 1, -2, 2, -3, 3, 4)
BIG_GRANT = 24 * 2**20


def cp_index(z, y, core):
    return ((z % N_Z) * N_Y + y % N_Y) * 2 + core


def cp_pairs(step):
    return [
        (cp_index(z, y, c), cp_index(z, y + step, c))
        for z in range(N_Z)
        for y in range(N_Y)
        for c in range(2)
    ]


CORE_PAIRS = [(i, i ^ 1) for i in range(N_CP)]
Z_GROUPS = [[cp_index(z, y, c) for z in range(N_Z)] for y in range(N_Y) for c in range(2)]
ZHI_PAIRS = [(i, (i + N_X) % N_TP) for i in range(N_TP)]


def x_pairs(step):
    return [(i, (i // N_X) * N_X + (i + step) % N_X) for i in range(N_TP)]


def angles_of(freq, first_run, second_run, rows):
    row = lax.broadcasted_iota(jnp.int32, (rows, HD), 0)
    pos = jnp.where(row < HALF, first_run * HALF + row, second_run * HALF + row - HALF)
    angles = pos.astype(jnp.float32) * freq
    low = lax.broadcasted_iota(jnp.int32, (rows, HD), 1) < HALF
    sin = jnp.sin(angles)
    return jnp.cos(angles), jnp.where(low, -sin, sin)


def turned(x, cos, sin):
    return x * cos + pltpu.roll(x, HALF, 1) * sin


SMEM = pl.BlockSpec(memory_space=pltpu.SMEM)
VMEM = pl.BlockSpec(memory_space=pltpu.VMEM)
ANY = pl.BlockSpec(memory_space=pl.ANY)


def coordinates():
    me = lax.axis_index("cp")
    return me, lax.div(me, 2 * N_Y), lax.rem(lax.div(me, 2), N_Y), lax.rem(me, 2)


def pack_kernel(positions, keys, values, freq, out):
    first = lax.div(positions[lax.axis_index("cp") * ROWS], HALF)
    cos, sin = angles_of(freq[...], first, RUNS - 1 - first, ROWS)
    k_rot = turned(keys[...].astype(jnp.float32), cos, sin).astype(jnp.bfloat16)
    out[0] = k_rot
    out[1] = values[...]


def pack(positions, keys, values):
    return pl.pallas_call(
        pack_kernel,
        out_shape=jax.ShapeDtypeStruct((2, ROWS, HD), jnp.bfloat16),
        in_specs=[SMEM, VMEM, VMEM, VMEM],
        out_specs=VMEM,
        cost_estimate=pl.CostEstimate(flops=1_000_000, bytes_accessed=400_000, transcendentals=0),
        name="pack",
    )(positions, keys, values, jnp.asarray(FREQ))


def turn_kernel(positions, queries, freq, unit, q_rot):
    del unit
    my_run = lax.div(positions[lax.axis_index("cp") * ROWS], HALF)
    cos, sin = angles_of(freq[...], my_run, RUNS - 1 - my_run, ROWS)
    for h in range(KVH):
        q = turned(queries[:, h * HD : (h + 1) * HD].astype(jnp.float32), cos, sin)
        q = q.astype(jnp.bfloat16)
        q_rot[0, h * HALF : (h + 1) * HALF, :] = q[:HALF]
        q_rot[1, h * HALF : (h + 1) * HALF, :] = q[HALF:]


def turn(positions, queries, unit):
    return pl.pallas_call(
        turn_kernel,
        out_shape=jax.ShapeDtypeStruct((2, KVH * HALF, HD), jnp.bfloat16),
        in_specs=[SMEM, VMEM, VMEM, ANY],
        out_specs=VMEM,
        compiler_params=pltpu.CompilerParams(vmem_limit_bytes=BIG_GRANT),
        cost_estimate=pl.CostEstimate(flops=2_000_000, bytes_accessed=600_000, transcendentals=0),
        name="turn",
    )(positions, queries, jnp.asarray(FREQ), unit)


LIST_ROWS = ((0, 1), (2, 3))
MISC = 4
AT_COUNT, AT_RUN = 0, 4


def clip_valid(counts, run):
    return jnp.clip(counts[lax.shift_right_logical(run, 1)] - (run & 1) * HALF, 0, HALF)


def lists_kernel(positions, counts, after, table):
    del after
    me, _, y_me, core = coordinates()
    my_run = lax.shift_right_logical(positions[me * ROWS], 6)
    places = [((y_me + (off + N_Y)) & (N_Y - 1)) * 2 for off in OFFSETS]

    for part in range(2):
        if part == 0:
            blocks = [(0, b) for b in range(FIRST)]
        else:
            blocks = [(0, b) for b in range(FIRST, SRC)] + [(1, b) for b in range(SRC)]
        n_low, n_high = jnp.int32(0), jnp.int32(0)
        low, high = LIST_ROWS[part]
        for b, (side, at) in enumerate(blocks):
            src = at % N_Z * 2 * N_Y + places[at // N_Z] + (core if side == 0 else 1 - core)
            run = lax.shift_right_logical(positions[src * ROWS], 6)
            first = b * 256 + clip_valid(counts, run)
            second = b * 256 + 128 + clip_valid(counts, RUNS - 1 - run)
            table[high, n_high] = first
            n_high = n_high + 1
            table[high, n_high] = second
            n_high = n_high + (run > my_run).astype(jnp.int32)
            table[low, n_low] = first
            n_low = n_low + (run < my_run).astype(jnp.int32)
        for r in range(16):
            table[low, n_low + r] = 0
            table[high, n_high + r] = 0
        table[MISC, AT_COUNT + low] = n_low
        table[MISC, AT_COUNT + high] = n_high
    table[MISC, AT_RUN] = my_run


def lists(positions, counts, after):
    return pl.pallas_call(
        lists_kernel,
        out_shape=jax.ShapeDtypeStruct((8, LANES), jnp.int32),
        in_specs=[SMEM, SMEM, ANY],
        out_specs=SMEM,
        compiler_params=pltpu.CompilerParams(vmem_limit_bytes=BIG_GRANT),
        cost_estimate=pl.CostEstimate(flops=2_000_000, bytes_accessed=300_000, transcendentals=0),
        name="lists",
    )(positions, counts, after)


AT_PICK, AT_PLACE = 0, 8


def route_kernel(positions, counts, owner_row, owner_col, owner_slot, after, table):
    del after
    me, _, y_me, core = coordinates()
    tp = lax.axis_index("tp")

    def page_of(head):
        page = jnp.int32(0)
        for p in range(N_CP):
            page = jnp.where(owner_row[head, p] == me, p, page)
        return page

    page = page_of(tp)
    for half in range(2):
        run = page * 2 + half
        second = run >= N_CP
        j = jnp.where(second, RUNS - 1 - run, run)
        src = jnp.int32(0)
        for s in range(N_CP):
            src = jnp.where(lax.shift_right_logical(positions[s * ROWS], 6) == j, s, src)
        off = (lax.shift_right_logical(src, 1) - y_me) & (N_Y - 1)
        order = jnp.where(off < N_Y // 2, 2 * off, 2 * (N_Y - off) - 1)
        at = AT_PICK + 4 * half
        table[at] = ((src & 1) != core).astype(jnp.int32)
        table[at + 1] = order * N_Z + lax.shift_right_logical(src, 4)
        table[at + 2] = second.astype(jnp.int32)
        table[at + 3] = clip_valid(counts, run)

    hi, x = lax.div(tp, N_X), lax.rem(tp, N_X)
    for i, step in enumerate((0, 1, -1, 2)):
        for d in range(2):
            head = lax.rem(hi + d, 2) * N_X + lax.rem(x - step + N_X, N_X)
            p = page_of(head)
            mine = owner_col[head, p] == tp
            table[AT_PLACE + i * 2 + d] = jnp.where(mine, owner_slot[head, p], -1)


def route(positions, counts, owner_row, owner_col, owner_slot, after):
    return pl.pallas_call(
        route_kernel,
        out_shape=jax.ShapeDtypeStruct((LANES,), jnp.int32),
        in_specs=[SMEM, SMEM, SMEM, SMEM, SMEM, ANY],
        out_specs=SMEM,
        compiler_params=pltpu.CompilerParams(vmem_limit_bytes=BIG_GRANT),
        cost_estimate=pl.CostEstimate(flops=2_000_000, bytes_accessed=300_000, transcendentals=0),
        name="route",
    )(positions, counts, owner_row, owner_col, owner_slot, after)


COLS = KVH * HALF
SCALE = math.log2(math.e) / math.sqrt(HD)
dot = functools.partial(lax.dot_general, preferred_element_type=jnp.float32)


def fold(q, keys, vals, bias, allowed, state):
    top, total, acc = state
    s = dot(keys, q, (((1,), (1,)), ((), ()))) * SCALE
    s = s + jnp.concatenate([bias] * (COLS // HD), axis=1)
    if allowed is not None:
        s = jnp.where(allowed, s, -BIG)
    new_top = jnp.maximum(top, jnp.max(s, axis=0, keepdims=True))
    factor = jnp.exp2(top - new_top)
    w = jnp.exp2(s - new_top)
    total = total * factor + jnp.sum(w, axis=0, keepdims=True)
    acc = acc * factor + dot(vals, w.astype(jnp.bfloat16), (((0,), (0,)), ((), ())))
    return new_top, total, acc


def bias_of(valid):
    return jnp.where(lax.broadcasted_iota(jnp.int32, (HALF, HD), 0) < valid, 0.0, -BIG)


def fold_list(table, row, q, kv, state):
    def chunk(size, start, state):
        ks, vs, biases = [], [], []
        for r in range(size):
            code = table[row, start + r]
            b = lax.shift_right_logical(code, 8)
            rows = pl.ds(pl.multiple_of(lax.shift_right_logical(code & 128, 1), HALF), HALF)
            ks.append(kv[b, 0, rows, :])
            vs.append(kv[b, 1, rows, :])
            biases.append(bias_of(code & 127))
        return fold(
            q,
            jnp.concatenate(ks, axis=0),
            jnp.concatenate(vs, axis=0),
            jnp.concatenate(biases, axis=0),
            None,
            state,
        )

    count = table[MISC, AT_COUNT + row]
    wide = lax.shift_right_logical(count + 7, 4)
    state = lax.fori_loop(0, wide, lambda i, st: chunk(16, i * 16, st), state)
    narrow = (count > wide * 16).astype(jnp.int32)
    return lax.fori_loop(0, narrow, lambda i, st: chunk(8, wide * 16, st), state)


def first_kernel(table, counts, q_rot, own, tops, totals, accs, kv, sem):
    copy = pltpu.make_async_copy(own, kv, sem)
    copy.start()
    _, z_me, _, _ = coordinates()
    my_run = table[MISC, AT_RUN]
    copy.wait()
    key = lax.broadcasted_iota(jnp.int32, (HALF, COLS), 0)
    row = lax.broadcasted_iota(jnp.int32, (HALF, COLS), 1) & (HALF - 1)
    for part in range(2):
        q = q_rot[part]
        state = (
            jnp.full((1, COLS), -BIG, jnp.float32),
            jnp.zeros((1, COLS), jnp.float32),
            jnp.zeros((HD, COLS), jnp.float32),
        )
        run = my_run if part == 0 else RUNS - 1 - my_run
        page = lax.shift_right_logical(run, 1)
        valid = jnp.clip(counts[page] - (run & 1) * HALF, 0, HALF)
        rows = slice(part * HALF, (part + 1) * HALF)
        state = fold(q, kv[z_me, 0, rows], kv[z_me, 1, rows], bias_of(valid), key <= row, state)
        state = fold_list(table, LIST_ROWS[0][part], q, kv, state)
        tops[part], totals[part], accs[part] = state


STATE = (
    jax.ShapeDtypeStruct((2, 1, COLS), jnp.float32),
    jax.ShapeDtypeStruct((2, 1, COLS), jnp.float32),
    jax.ShapeDtypeStruct((2, HD, COLS), jnp.float32),
)


def attend_first(table, counts, q_rot, own):
    return pl.pallas_call(
        first_kernel,
        out_shape=STATE,
        in_specs=[SMEM, SMEM, VMEM, ANY],
        out_specs=(VMEM, VMEM, VMEM),
        scratch_shapes=[
            pltpu.VMEM((FIRST, 2, ROWS, HD), jnp.bfloat16),
            pltpu.SemaphoreType.DMA,
        ],
        compiler_params=pltpu.CompilerParams(vmem_limit_bytes=BIG_GRANT),
        cost_estimate=pl.CostEstimate(
            flops=6_000_000_000, bytes_accessed=3_000_000, transcendentals=2_000_000
        ),
        name="attend_first",
    )(table, counts, q_rot, own)


def rest_kernel(table, q_rot, tops, totals, accs, own, other, out, kv, sems):
    copies = [
        pltpu.make_async_copy(
            own.at[pl.ds(FIRST, SRC - FIRST)], kv.at[pl.ds(0, SRC - FIRST)], sems.at[0]
        ),
        pltpu.make_async_copy(other, kv.at[pl.ds(SRC - FIRST, SRC)], sems.at[1]),
    ]
    for copy in copies:
        copy.start()
    for copy in copies:
        copy.wait()
    for part in range(2):
        state = tops[part], totals[part], accs[part]
        _, total, acc = fold_list(table, LIST_ROWS[1][part], q_rot[part], kv, state)
        res = jnp.transpose(acc / total).astype(jnp.bfloat16)
        for h in range(KVH):
            out[part * HALF : (part + 1) * HALF, h * HD : (h + 1) * HD] = res[
                h * HALF : (h + 1) * HALF
            ]


def attend_rest(table, q_rot, state, own, other):
    return pl.pallas_call(
        rest_kernel,
        out_shape=jax.ShapeDtypeStruct((ROWS, KVH * HD), jnp.bfloat16),
        in_specs=[SMEM, VMEM, VMEM, VMEM, VMEM, ANY, ANY],
        out_specs=VMEM,
        scratch_shapes=[
            pltpu.VMEM((REST, 2, ROWS, HD), jnp.bfloat16),
            pltpu.SemaphoreType.DMA((2,)),
        ],
        compiler_params=pltpu.CompilerParams(vmem_limit_bytes=BIG_GRANT),
        cost_estimate=pl.CostEstimate(
            flops=8_000_000_000, bytes_accessed=4_000_000, transcendentals=2_000_000
        ),
        name="attend_rest",
    )(table, q_rot, *state, own, other)


def pick_kernel(table, own, other, out, near, held, sems):
    for half in range(2):
        at = AT_PICK + 4 * half
        side, index, second = (table[at + i] for i in range(3))
        rows = pl.ds(pl.multiple_of(second * HALF, HALF), HALF)
        for is_other, blocks in ((0, own), (1, other)):

            @pl.when(side == is_other)
            def _(blocks=blocks, half=half, index=index, rows=rows):
                pltpu.make_async_copy(
                    blocks.at[index, :, rows], held.at[half], sems.at[half]
                ).start()

    row = lax.broadcasted_iota(jnp.int32, (HALF, HD), 0)
    for half in range(2):
        pltpu.make_async_copy(own.at[0, :, pl.ds(0, HALF)], held.at[half], sems.at[half]).wait()
        keep = row < table[AT_PICK + 4 * half + 3]
        for i in range(2):
            block = jnp.where(keep, held[half, i].astype(jnp.float32), 0.0).astype(jnp.bfloat16)
            out[i, half * HALF : (half + 1) * HALF, :] = block
            near[0, i, half * HALF : (half + 1) * HALF, :] = block


def pick(table, own, other):
    return pl.pallas_call(
        pick_kernel,
        out_shape=(
            jax.ShapeDtypeStruct((2, PAGE, HD), jnp.bfloat16),
            jax.ShapeDtypeStruct((2, 2, PAGE, HD), jnp.bfloat16),
        ),
        in_specs=[SMEM, ANY, ANY],
        out_specs=(VMEM, VMEM),
        scratch_shapes=[
            pltpu.VMEM((2, 2, HALF, HD), jnp.bfloat16),
            pltpu.SemaphoreType.DMA((2,)),
        ],
        compiler_params=pltpu.CompilerParams(vmem_limit_bytes=BIG_GRANT),
        cost_estimate=pl.CostEstimate(flops=100_000, bytes_accessed=300_000, transcendentals=0),
        name="pick",
    )(table, own, other)


def place_kernel(table, near, right, left, far, pool_k, pool_v, sems):
    for slot in range(2):
        empty = True
        for i, pages in enumerate((near, right, left, far)):
            for hi in range(2):
                hit = table[AT_PLACE + i * 2 + hi] == slot
                empty = jnp.logical_and(empty, jnp.logical_not(hit))

                @pl.when(hit)
                def _(pages=pages, hi=hi, slot=slot):
                    pltpu.make_async_copy(pages.at[hi, 0], pool_k.at[slot], sems.at[slot, 0]).start()
                    pltpu.make_async_copy(pages.at[hi, 1], pool_v.at[slot], sems.at[slot, 1]).start()

        @pl.when(empty)
        def _(slot=slot):
            pool_k[slot] = jnp.zeros((PAGE, HD), jnp.bfloat16)
            pool_v[slot] = jnp.zeros((PAGE, HD), jnp.bfloat16)

        @pl.when(jnp.logical_not(empty))
        def _(slot=slot):
            pltpu.make_async_copy(near.at[0, 0], pool_k.at[slot], sems.at[slot, 0]).wait()
            pltpu.make_async_copy(near.at[0, 1], pool_v.at[slot], sems.at[slot, 1]).wait()


def place(table, near, right, left, far):
    shape = jax.ShapeDtypeStruct((2, PAGE, HD), jnp.bfloat16)
    return pl.pallas_call(
        place_kernel,
        out_shape=(shape, shape),
        in_specs=[SMEM, ANY, ANY, ANY, ANY],
        out_specs=(VMEM, VMEM),
        scratch_shapes=[pltpu.SemaphoreType.DMA((2, 2))],
        compiler_params=pltpu.CompilerParams(vmem_limit_bytes=BIG_GRANT),
        cost_estimate=pl.CostEstimate(flops=100_000, bytes_accessed=800_000, transcendentals=0),
        name="place",
    )(table, near, right, left, far)


def shards(queries, keys, values, positions, counts, owner_row, owner_col, owner_slot):
    tie = lax.optimization_barrier
    ahead, back = cp_pairs(1), cp_pairs(-1)
    packed = pack(positions, keys, values)
    spread = jnp.broadcast_to(packed, (N_Z, 2, ROWS, HD))
    unit = lax.all_to_all(spread, "cp", 0, 0, axis_index_groups=Z_GROUPS)

    f1 = lax.ppermute(unit, "cp", ahead)
    b1 = lax.ppermute(unit, "cp", back)
    f1, q_rot = tie((f1, turn(positions, queries, unit)))
    f2 = lax.ppermute(f1, "cp", ahead)
    b2 = lax.ppermute(b1, "cp", back)
    f2, table = tie((f2, lists(positions, counts, f1)))
    f3 = lax.ppermute(f2, "cp", ahead)
    b3 = lax.ppermute(b2, "cp", back)
    f3, routes = tie((f3, route(positions, counts, owner_row, owner_col, owner_slot, f2)))
    f4 = lax.ppermute(f3, "cp", ahead)
    state = attend_first(
        table, counts, q_rot, jnp.concatenate([unit, f1, b1, f2, b2, f3, b3], axis=0)
    )
    f4, state = tie((f4, state))
    own = jnp.concatenate([unit, f1, b1, f2, b2, f3, b3, f4], axis=0)
    other = lax.ppermute(own, "cp", CORE_PAIRS)

    picked, near = pick(routes, own, other)
    across = lax.ppermute(picked, "tp", ZHI_PAIRS)
    attended = attend_rest(table, q_rot, state, own, other)
    across, attended = tie((across, attended))
    near = lax.dynamic_update_slice(near, across[None], (1, 0, 0, 0))
    right = lax.ppermute(near, "tp", x_pairs(1))
    left = lax.ppermute(near, "tp", x_pairs(-1))
    far = lax.ppermute(near, "tp", x_pairs(2))
    pool_keys, pool_values = place(routes, near, right, left, far)
    return attended, pool_keys, pool_values


def solution(mesh):
    return jax.shard_map(
        shards,
        mesh=mesh,
        in_specs=(P("cp", "tp"), P("cp", "tp"), P("cp", "tp"), P(), P(), P(), P(), P()),
        out_specs=(P("cp", "tp"), P(("cp", "tp"), None, None), P(("cp", "tp"), None, None)),
        check_vma=False,
    )
```

```python
import functools
import math

import jax
import jax.numpy as jnp
import numpy as np
from jax import lax
from jax.experimental import pallas as pl
from jax.experimental.pallas import tpu as pltpu
from jax.sharding import PartitionSpec as P

KVH = 8
HD = 128
PAGE = 128
HALF = 64
ROWS = 128
N_CP = 64
N_Z = 4
N_Y = 8
N_TP = 8
N_X = 4
SRC = N_CP // 2
LANES = 128
RUNS = 2 * N_CP
BIG = 1e30

THETA = 500000.0
FREQ = np.concatenate([THETA ** (-np.arange(HALF) * 2.0 / HD)] * 2).astype(np.float32)[None, :]
OFFSETS = (0, -1, 1, -2, 2, -3, 3, 4)
EARLY = 20
LATE = SRC - EARLY
FIRST = 28
REST = N_CP - FIRST
BIG_GRANT = 24 * 2**20


def cp_index(z, y, core):
    return ((z % N_Z) * N_Y + y % N_Y) * 2 + core


def y_pairs(step):
    return [
        (cp_index(z, y, c), cp_index(z, y + step, c))
        for z in range(N_Z)
        for y in range(N_Y)
        for c in range(2)
    ]


Z_GROUPS = [[cp_index(z, y, c) for z in range(N_Z)] for y in range(N_Y) for c in range(2)]
X_GROUPS = [[hi * N_X + x for x in range(N_X)] for hi in range(2)]
CORE_PAIRS = [(i, i ^ 1) for i in range(N_CP)]
ZHI_PAIRS = [(i, (i + N_X) % N_TP) for i in range(N_TP)]


def angles_of(freq, first_run, second_run, rows):
    row = lax.broadcasted_iota(jnp.int32, (rows, HD), 0)
    pos = jnp.where(row < HALF, first_run * HALF + row, second_run * HALF + row - HALF)
    angles = pos.astype(jnp.float32) * freq
    low = lax.broadcasted_iota(jnp.int32, (rows, HD), 1) < HALF
    sin = jnp.sin(angles)
    return jnp.cos(angles), jnp.where(low, -sin, sin)


def turned(x, cos, sin):
    return x * cos + pltpu.roll(x, HALF, 1) * sin


SMEM = pl.BlockSpec(memory_space=pltpu.SMEM)
VMEM = pl.BlockSpec(memory_space=pltpu.VMEM)
ANY = pl.BlockSpec(memory_space=pl.ANY)


def coordinates():
    me = lax.axis_index("cp")
    return me, lax.div(me, 2 * N_Y), lax.rem(lax.div(me, 2), N_Y), lax.rem(me, 2)


def pack_kernel(positions, keys, values, freq, out):
    first = lax.div(positions[lax.axis_index("cp") * ROWS], HALF)
    cos, sin = angles_of(freq[...], first, RUNS - 1 - first, ROWS)
    k_rot = turned(keys[...].astype(jnp.float32), cos, sin).astype(jnp.bfloat16)
    v = values[...]
    for i in range(N_Z):
        out[i, 0] = k_rot
        out[i, 1] = v


def pack(positions, keys, values):
    return pl.pallas_call(
        pack_kernel,
        out_shape=jax.ShapeDtypeStruct((N_Z, 2, ROWS, HD), jnp.bfloat16),
        in_specs=[SMEM, VMEM, VMEM, VMEM],
        out_specs=VMEM,
        cost_estimate=pl.CostEstimate(flops=1_000_000, bytes_accessed=400_000, transcendentals=0),
        name="pack",
    )(positions, keys, values, jnp.asarray(FREQ))


def turn_kernel(positions, queries, freq, after, q_rot, runs):
    del after
    for s in range(N_CP):
        runs[s] = lax.shift_right_logical(positions[s * ROWS], 6)
    my_run = runs[lax.axis_index("cp")]
    cos, sin = angles_of(freq[...], my_run, RUNS - 1 - my_run, ROWS)
    for h in range(KVH):
        q = turned(queries[:, h * HD : (h + 1) * HD].astype(jnp.float32), cos, sin)
        q = q.astype(jnp.bfloat16)
        q_rot[0, h * HALF : (h + 1) * HALF, :] = q[:HALF]
        q_rot[1, h * HALF : (h + 1) * HALF, :] = q[HALF:]


def turn(positions, queries, after):
    return pl.pallas_call(
        turn_kernel,
        out_shape=(
            jax.ShapeDtypeStruct((2, KVH * HALF, HD), jnp.bfloat16),
            jax.ShapeDtypeStruct((N_CP,), jnp.int32),
        ),
        in_specs=[SMEM, VMEM, VMEM, ANY],
        out_specs=(VMEM, SMEM),
        compiler_params=pltpu.CompilerParams(vmem_limit_bytes=BIG_GRANT),
        cost_estimate=pl.CostEstimate(flops=2_000_000, bytes_accessed=600_000, transcendentals=0),
        name="turn",
    )(positions, queries, jnp.asarray(FREQ), after)


LIST_ROWS = ((0, 1), (2, 3))
MISC = 4
AT_COUNT, AT_RUN, AT_PICK = 0, 4, 8


def clip_valid(counts, run):
    return jnp.clip(counts[lax.shift_right_logical(run, 1)] - (run & 1) * HALF, 0, HALF)


def page_of(owner_row, head, me):
    page = jnp.int32(0)
    for p in range(N_CP):
        page = jnp.where(owner_row[head, p] == me, p, page)
    return page


def lists_kernel(runs, counts, owner_row, after, table):
    del after
    me, z_me, y_me, core = coordinates()
    my_run = runs[me]

    for part in range(2):
        if part == 0:
            blocks = [(0, b) for b in range(FIRST)]
        else:
            blocks = [(0, b) for b in range(FIRST, SRC)] + [(1, b) for b in range(SRC)]
        n_low, n_high = jnp.int32(0), jnp.int32(0)
        low, high = LIST_ROWS[part]
        for b, (side, at) in enumerate(blocks):
            src_y = (y_me + OFFSETS[at // N_Z]) & (N_Y - 1)
            src_core = core if side == 0 else 1 - core
            run = runs[((at % N_Z)) * 2 * N_Y + src_y * 2 + src_core]
            first = b * 256 + clip_valid(counts, run)
            second = b * 256 + 128 + clip_valid(counts, RUNS - 1 - run)
            table[high, n_high] = first
            n_high = n_high + 1
            table[high, n_high] = second
            n_high = n_high + (run > my_run).astype(jnp.int32)
            table[low, n_low] = first
            n_low = n_low + (run < my_run).astype(jnp.int32)
        for r in range(16):
            table[low, n_low + r] = 0
            table[high, n_high + r] = 0
        table[MISC, AT_COUNT + low] = n_low
        table[MISC, AT_COUNT + high] = n_high
    table[MISC, AT_RUN] = my_run

    page = page_of(owner_row, lax.axis_index("tp"), me)
    for half in range(2):
        run = page * 2 + half
        second = run >= N_CP
        j = jnp.where(second, RUNS - 1 - run, run)
        src = jnp.int32(0)
        for s in range(N_CP):
            src = jnp.where(runs[s] == j, s, src)
        src_core = src & 1
        off = (lax.shift_right_logical(src, 1) - y_me) & (N_Y - 1)
        order = jnp.where(off < N_Y // 2, 2 * off, 2 * (N_Y - off) - 1)
        at = AT_PICK + 4 * half
        table[MISC, at] = (src_core != core).astype(jnp.int32)
        table[MISC, at + 1] = order * N_Z + (lax.shift_right_logical(src, 4))
        table[MISC, at + 2] = second.astype(jnp.int32)
        table[MISC, at + 3] = clip_valid(counts, run)


def lists(runs, counts, owner_row, after):
    return pl.pallas_call(
        lists_kernel,
        out_shape=jax.ShapeDtypeStruct((8, LANES), jnp.int32),
        in_specs=[SMEM, SMEM, SMEM, ANY],
        out_specs=SMEM,
        compiler_params=pltpu.CompilerParams(vmem_limit_bytes=BIG_GRANT),
        cost_estimate=pl.CostEstimate(flops=2_000_000, bytes_accessed=300_000, transcendentals=0),
        name="lists",
    )(runs, counts, owner_row, after)


def route_kernel(owner_row, owner_col, owner_slot, after, table):
    del after
    me = lax.axis_index("cp")
    tp = lax.axis_index("tp")
    for i in range(N_X):
        for d in range(2):
            head = i + ((tp & N_X) ^ (d * N_X))
            p = page_of(owner_row, head, me)
            mine = owner_col[head, p] == tp
            table[i * 2 + d] = jnp.where(mine, owner_slot[head, p], -1)


def route(owner_row, owner_col, owner_slot, after):
    return pl.pallas_call(
        route_kernel,
        out_shape=jax.ShapeDtypeStruct((8,), jnp.int32),
        in_specs=[SMEM, SMEM, SMEM, ANY],
        out_specs=SMEM,
        compiler_params=pltpu.CompilerParams(vmem_limit_bytes=BIG_GRANT),
        cost_estimate=pl.CostEstimate(flops=2_000_000, bytes_accessed=300_000, transcendentals=0),
        name="route",
    )(owner_row, owner_col, owner_slot, after)


COLS = KVH * HALF
SCALE = math.log2(math.e) / math.sqrt(HD)
dot = functools.partial(lax.dot_general, preferred_element_type=jnp.float32)


def fold(q, keys, vals, bias, allowed, state):
    top, total, acc = state
    s = dot(keys, q, (((1,), (1,)), ((), ()))) * SCALE
    s = s + jnp.concatenate([bias] * (COLS // HD), axis=1)
    if allowed is not None:
        s = jnp.where(allowed, s, -BIG)
    new_top = jnp.maximum(top, jnp.max(s, axis=0, keepdims=True))
    factor = jnp.exp2(top - new_top)
    w = jnp.exp2(s - new_top)
    total = total * factor + jnp.sum(w, axis=0, keepdims=True)
    acc = acc * factor + dot(vals, w.astype(jnp.bfloat16), (((0,), (0,)), ((), ())))
    return new_top, total, acc


def bias_of(valid):
    return jnp.where(lax.broadcasted_iota(jnp.int32, (HALF, HD), 0) < valid, 0.0, -BIG)


def fold_list(table, row, q, kv, state):
    def chunk(size, start, state):
        ks, vs, biases = [], [], []
        for r in range(size):
            code = table[row, start + r]
            b = lax.shift_right_logical(code, 8)
            rows = pl.ds(pl.multiple_of(lax.shift_right_logical(code & 128, 1), HALF), HALF)
            ks.append(kv[b, 0, rows, :])
            vs.append(kv[b, 1, rows, :])
            biases.append(bias_of(code & 127))
        return fold(
            q,
            jnp.concatenate(ks, axis=0),
            jnp.concatenate(vs, axis=0),
            jnp.concatenate(biases, axis=0),
            None,
            state,
        )

    count = table[MISC, AT_COUNT + row]
    wide = lax.shift_right_logical(count + 7, 4)
    state = lax.fori_loop(0, wide, lambda i, st: chunk(16, i * 16, st), state)
    narrow = (count > wide * 16).astype(jnp.int32)
    return lax.fori_loop(0, narrow, lambda i, st: chunk(8, wide * 16, st), state)


def copy_blocks(pieces, kv, sems):
    copies, at = [], 0
    for i, piece in enumerate(pieces):
        size = piece.shape[0]
        copies.append(pltpu.make_async_copy(piece, kv.at[pl.ds(at, size)], sems.at[i]))
        at += size
    for copy in copies:
        copy.start()
    for copy in copies:
        copy.wait()


def first_kernel(table, counts, q_rot, early, f3, b3, tops, totals, accs, kv, sems):
    copy_blocks((early, f3, b3), kv, sems)
    _, z_me, _, _ = coordinates()
    my_run = table[MISC, AT_RUN]
    key = lax.broadcasted_iota(jnp.int32, (HALF, COLS), 0)
    row = lax.broadcasted_iota(jnp.int32, (HALF, COLS), 1) & (HALF - 1)
    for part in range(2):
        q = q_rot[part]
        state = (
            jnp.full((1, COLS), -BIG, jnp.float32),
            jnp.zeros((1, COLS), jnp.float32),
            jnp.zeros((HD, COLS), jnp.float32),
        )
        run = my_run if part == 0 else RUNS - 1 - my_run
        page = lax.shift_right_logical(run, 1)
        valid = jnp.clip(counts[page] - (run & 1) * HALF, 0, HALF)
        rows = slice(part * HALF, (part + 1) * HALF)
        state = fold(q, kv[z_me, 0, rows], kv[z_me, 1, rows], bias_of(valid), key <= row, state)
        state = fold_list(table, LIST_ROWS[0][part], q, kv, state)
        tops[part], totals[part], accs[part] = state


STATE = (
    jax.ShapeDtypeStruct((2, 1, COLS), jnp.float32),
    jax.ShapeDtypeStruct((2, 1, COLS), jnp.float32),
    jax.ShapeDtypeStruct((2, HD, COLS), jnp.float32),
)


def attend_first(table, counts, q_rot, early, f3, b3):
    return pl.pallas_call(
        first_kernel,
        out_shape=STATE,
        in_specs=[SMEM, SMEM, VMEM, ANY, ANY, ANY],
        out_specs=(VMEM, VMEM, VMEM),
        scratch_shapes=[
            pltpu.VMEM((FIRST, 2, ROWS, HD), jnp.bfloat16),
            pltpu.SemaphoreType.DMA((3,)),
        ],
        compiler_params=pltpu.CompilerParams(vmem_limit_bytes=BIG_GRANT),
        cost_estimate=pl.CostEstimate(
            flops=6_000_000_000, bytes_accessed=3_000_000, transcendentals=2_000_000
        ),
        name="attend_first",
    )(table, counts, q_rot, early, f3, b3)


def rest_kernel(table, q_rot, tops, totals, accs, f4, early, late, out, kv, sems):
    copy_blocks((f4, early, late), kv, sems)
    for part in range(2):
        state = tops[part], totals[part], accs[part]
        _, total, acc = fold_list(table, LIST_ROWS[1][part], q_rot[part], kv, state)
        res = jnp.transpose(acc / total).astype(jnp.bfloat16)
        for h in range(KVH):
            out[part * HALF : (part + 1) * HALF, h * HD : (h + 1) * HD] = res[
                h * HALF : (h + 1) * HALF
            ]


def attend_rest(table, q_rot, state, f4, early, late):
    return pl.pallas_call(
        rest_kernel,
        out_shape=jax.ShapeDtypeStruct((ROWS, KVH * HD), jnp.bfloat16),
        in_specs=[SMEM, VMEM, VMEM, VMEM, VMEM, ANY, ANY, ANY],
        out_specs=VMEM,
        scratch_shapes=[
            pltpu.VMEM((REST, 2, ROWS, HD), jnp.bfloat16),
            pltpu.SemaphoreType.DMA((3,)),
        ],
        compiler_params=pltpu.CompilerParams(vmem_limit_bytes=BIG_GRANT),
        cost_estimate=pl.CostEstimate(
            flops=8_000_000_000, bytes_accessed=4_000_000, transcendentals=2_000_000
        ),
        name="attend_rest",
    )(table, q_rot, *state, f4, early, late)


def pick_kernel(table, own_early, own_late, other_early, other_late, out, held, sems):
    for half in range(2):
        at = AT_PICK + 4 * half
        side, index, second = (table[MISC, at + i] for i in range(3))
        rows = pl.ds(pl.multiple_of(second * HALF, HALF), HALF)
        for is_other, early, late in ((0, own_early, own_late), (1, other_early, other_late)):

            @pl.when((side == is_other) & (index < EARLY))
            def _(early=early, half=half, index=index, rows=rows):
                pltpu.make_async_copy(
                    early.at[index, :, rows], held.at[half], sems.at[half]
                ).start()

            @pl.when((side == is_other) & (index >= EARLY))
            def _(late=late, half=half, index=index, rows=rows):
                pltpu.make_async_copy(
                    late.at[index - EARLY, :, rows], held.at[half], sems.at[half]
                ).start()

    row = lax.broadcasted_iota(jnp.int32, (HALF, HD), 0)
    for half in range(2):
        pltpu.make_async_copy(own_late.at[0, :, pl.ds(0, HALF)], held.at[half], sems.at[half]).wait()
        keep = row < table[MISC, AT_PICK + 4 * half + 3]
        for i in range(2):
            block = jnp.where(keep, held[half, i].astype(jnp.float32), 0.0).astype(jnp.bfloat16)
            out[i, half * HALF : (half + 1) * HALF, :] = block


def pick(table, own_early, own_late, other_early, other_late):
    return pl.pallas_call(
        pick_kernel,
        out_shape=jax.ShapeDtypeStruct((2, PAGE, HD), jnp.bfloat16),
        in_specs=[SMEM, ANY, ANY, ANY, ANY],
        out_specs=VMEM,
        scratch_shapes=[
            pltpu.VMEM((2, 2, HALF, HD), jnp.bfloat16),
            pltpu.SemaphoreType.DMA((2,)),
        ],
        compiler_params=pltpu.CompilerParams(vmem_limit_bytes=BIG_GRANT),
        cost_estimate=pl.CostEstimate(flops=100_000, bytes_accessed=300_000, transcendentals=0),
        name="pick",
    )(table, own_early, own_late, other_early, other_late)


def place_kernel(table, pages, pool_k, pool_v, sems):
    for slot in range(2):
        empty = True
        for i in range(N_X):
            for hi in range(2):
                hit = table[i * 2 + hi] == slot
                empty = jnp.logical_and(empty, jnp.logical_not(hit))

                @pl.when(hit)
                def _(i=i, hi=hi, slot=slot):
                    pltpu.make_async_copy(pages.at[i, hi, 0], pool_k.at[slot], sems.at[slot, 0]).start()
                    pltpu.make_async_copy(pages.at[i, hi, 1], pool_v.at[slot], sems.at[slot, 1]).start()

        @pl.when(empty)
        def _(slot=slot):
            pool_k[slot] = jnp.zeros((PAGE, HD), jnp.bfloat16)
            pool_v[slot] = jnp.zeros((PAGE, HD), jnp.bfloat16)

        @pl.when(jnp.logical_not(empty))
        def _(slot=slot):
            pltpu.make_async_copy(pages.at[0, 0, 0], pool_k.at[slot], sems.at[slot, 0]).wait()
            pltpu.make_async_copy(pages.at[0, 0, 1], pool_v.at[slot], sems.at[slot, 1]).wait()


def place(table, pages):
    shape = jax.ShapeDtypeStruct((2, PAGE, HD), jnp.bfloat16)
    return pl.pallas_call(
        place_kernel,
        out_shape=(shape, shape),
        in_specs=[SMEM, ANY],
        out_specs=(VMEM, VMEM),
        scratch_shapes=[pltpu.SemaphoreType.DMA((2, 2))],
        compiler_params=pltpu.CompilerParams(vmem_limit_bytes=BIG_GRANT),
        cost_estimate=pl.CostEstimate(flops=100_000, bytes_accessed=800_000, transcendentals=0),
        name="place",
    )(table, pages)


def shards(queries, keys, values, positions, counts, owner_row, owner_col, owner_slot):
    tie = lax.optimization_barrier
    spread = pack(positions, keys, values)
    unit = lax.all_to_all(spread, "cp", 0, 0, axis_index_groups=Z_GROUPS)

    ahead, back = y_pairs(1), y_pairs(-1)
    f1 = lax.ppermute(unit, "cp", ahead)
    b1 = lax.ppermute(unit, "cp", back)
    f1, q_rot, runs = tie((f1, *turn(positions, queries, unit)))
    f2 = lax.ppermute(f1, "cp", ahead)
    b2 = lax.ppermute(b1, "cp", back)
    f2, table = tie((f2, lists(runs, counts, owner_row, f1)))
    f3 = lax.ppermute(f2, "cp", ahead)
    b3 = lax.ppermute(b2, "cp", back)
    own_early = jnp.concatenate([unit, f1, b1, f2, b2], axis=0)
    other_early = lax.ppermute(own_early, "cp", CORE_PAIRS)
    f4 = lax.ppermute(f3, "cp", ahead)
    state = attend_first(table, counts, q_rot, own_early, f3, b3)
    f4, state = tie((f4, state))
    own_late = jnp.concatenate([f3, b3, f4], axis=0)
    other_late = lax.ppermute(own_late, "cp", CORE_PAIRS)
    other_late, routes = tie((other_late, route(owner_row, owner_col, owner_slot, f4)))

    picked = pick(table, own_early, own_late, other_early, other_late)
    across = lax.ppermute(picked, "tp", ZHI_PAIRS)
    attended = attend_rest(table, q_rot, state, f4, other_early, other_late)
    across, attended = tie((across, attended))
    near = jnp.broadcast_to(jnp.stack([picked, across]), (N_X, 2, 2, PAGE, HD))
    pages = lax.all_to_all(near, "tp", 0, 0, axis_index_groups=X_GROUPS)
    pool_keys, pool_values = place(routes, pages)
    return attended, pool_keys, pool_values


def solution(mesh):
    return jax.shard_map(
        shards,
        mesh=mesh,
        in_specs=(P("cp", "tp"), P("cp", "tp"), P("cp", "tp"), P(), P(), P(), P(), P()),
        out_specs=(P("cp", "tp"), P(("cp", "tp"), None, None), P(("cp", "tp"), None, None)),
        check_vma=False,
    )
```

```python
import functools
import math

import jax
import jax.numpy as jnp
import numpy as np
from jax import lax
from jax.experimental import pallas as pl
from jax.experimental.pallas import tpu as pltpu
from jax.sharding import PartitionSpec as P

KVH = 8
HD = 128
PAGE = 128
HALF = 64
ROWS = 128
N_CP = 64
N_Z = 4
N_Y = 8
N_TP = 8
N_X = 4
SRC = N_CP // 2
LANES = 128
RUNS = 2 * N_CP
BIG = 1e30

THETA = 500000.0
RATES = THETA ** (-np.arange(HALF) * 2.0 / HD)


def cos_sin(positions):
    angles = np.asarray(positions)[:, None] * np.concatenate([RATES, RATES])[None, :]
    return np.stack([np.cos(angles), np.sin(angles)]).astype(np.float32)


RUN_TABLE = cos_sin(np.arange(RUNS) * HALF)
STEP_TABLE = cos_sin(np.arange(HALF))


OFFSETS = (0, -1, 1, -2, 2, -3, 3, 4)
EARLY = 20
LATE = SRC - EARLY
FIRST = 28
MIDDLE = 8
REST = N_CP - FIRST - MIDDLE
BIG_GRANT = 24 * 2**20


def cp_index(z, y, core):
    return ((z % N_Z) * N_Y + y % N_Y) * 2 + core


def y_pairs(step):
    return [
        (cp_index(z, y, c), cp_index(z, y + step, c))
        for z in range(N_Z)
        for y in range(N_Y)
        for c in range(2)
    ]


Z_GROUPS = [[cp_index(z, y, c) for z in range(N_Z)] for y in range(N_Y) for c in range(2)]
X_GROUPS = [[hi * N_X + x for x in range(N_X)] for hi in range(2)]
CORE_PAIRS = [(i, i ^ 1) for i in range(N_CP)]
MIRROR_PAIRS = [
    (cp_index(z, y, c) * N_TP + tp, cp_index(N_Z - 1 - z, y, c) * N_TP + (tp ^ N_X))
    for z in range(N_Z)
    for y in range(N_Y)
    for c in range(2)
    for tp in range(N_TP)
]


def angles_of(run_table, step_table, first_run):
    low = lax.broadcasted_iota(jnp.int32, (HALF, HD), 1) < HALF
    cos, sin = [], []
    for run in (first_run, RUNS - 1 - first_run):
        run_cos, run_sin = run_table[0, pl.ds(run, 1), :], run_table[1, pl.ds(run, 1), :]
        cos.append(run_cos * step_table[0] - run_sin * step_table[1])
        part = run_sin * step_table[0] + run_cos * step_table[1]
        sin.append(jnp.where(low, -part, part))
    return jnp.concatenate(cos, axis=0), jnp.concatenate(sin, axis=0)


def turned(x, cos, sin):
    return x * cos + pltpu.roll(x, HALF, 1) * sin


SMEM = pl.BlockSpec(memory_space=pltpu.SMEM)
VMEM = pl.BlockSpec(memory_space=pltpu.VMEM)
ANY = pl.BlockSpec(memory_space=pl.ANY)


def coordinates():
    me = lax.axis_index("cp")
    return me, lax.div(me, 2 * N_Y), lax.rem(lax.div(me, 2), N_Y), lax.rem(me, 2)


def pack_kernel(positions, keys, values, run_table, step_table, out):
    first = lax.shift_right_logical(positions[lax.axis_index("cp") & 7, 0], 6)
    cos, sin = angles_of(run_table, step_table, first)
    k_rot = turned(keys[...].astype(jnp.float32), cos, sin).astype(jnp.bfloat16)
    v = values[...]
    for i in range(N_Z):
        out[i, 0] = k_rot
        out[i, 1] = v


def pack(positions, keys, values):
    def whole(*shape):
        return pl.BlockSpec(shape, lambda i: (0,) * len(shape))

    return pl.pallas_call(
        pack_kernel,
        grid=(1,),
        out_shape=jax.ShapeDtypeStruct((N_Z, 2, ROWS, HD), jnp.bfloat16),
        in_specs=[
            pl.BlockSpec(
                (8, ROWS),
                lambda i: (lax.div(lax.axis_index("cp"), 8), 0),
                memory_space=pltpu.SMEM,
            ),
            whole(ROWS, HD),
            whole(ROWS, HD),
            whole(2, RUNS, HD),
            whole(2, HALF, HD),
        ],
        out_specs=whole(N_Z, 2, ROWS, HD),
        cost_estimate=pl.CostEstimate(flops=1_000_000, bytes_accessed=400_000, transcendentals=0),
        name="pack",
    )(positions.reshape(N_CP, ROWS), keys, values, jnp.asarray(RUN_TABLE), jnp.asarray(STEP_TABLE))


def turn_kernel(positions, queries, run_table, step_table, q_rot, runs):
    for s in range(N_CP):
        runs[s] = lax.shift_right_logical(positions[s * ROWS], 6)
    my_run = runs[lax.axis_index("cp")]
    cos, sin = angles_of(run_table, step_table, my_run)
    for h in range(KVH):
        q = turned(queries[:, h * HD : (h + 1) * HD].astype(jnp.float32), cos, sin)
        q = q.astype(jnp.bfloat16)
        q_rot[0, h * HALF : (h + 1) * HALF, :] = q[:HALF]
        q_rot[1, h * HALF : (h + 1) * HALF, :] = q[HALF:]


def turn(positions, queries):
    return pl.pallas_call(
        turn_kernel,
        out_shape=(
            jax.ShapeDtypeStruct((2, KVH * HALF, HD), jnp.bfloat16),
            jax.ShapeDtypeStruct((N_CP,), jnp.int32),
        ),
        in_specs=[SMEM, VMEM, VMEM, VMEM],
        out_specs=(VMEM, SMEM),
        compiler_params=pltpu.CompilerParams(vmem_limit_bytes=BIG_GRANT),
        cost_estimate=pl.CostEstimate(flops=2_000_000, bytes_accessed=600_000, transcendentals=0),
        name="turn",
    )(positions, queries, jnp.asarray(RUN_TABLE), jnp.asarray(STEP_TABLE))


LIST_ROWS = ((0, 1), (2, 3), (4, 5))
MISC = 6
AT_COUNT, AT_RUN = 0, 8
BLOCKS = 7


def clip_valid(counts, run):
    return jnp.clip(counts[lax.shift_right_logical(run, 1)] - (run & 1) * HALF, 0, HALF)


def lists_kernel(runs, counts, table):
    me, _, y_me, core = coordinates()
    my_run = runs[me]

    for part in range(3):
        if part == 0:
            blocks = [(0, b) for b in range(FIRST)]
        elif part == 1:
            blocks = [(1, b) for b in range(MIDDLE)]
        else:
            blocks = [(0, b) for b in range(FIRST, SRC)] + [(1, b) for b in range(MIDDLE, SRC)]
        n_low, n_high = jnp.int32(0), jnp.int32(0)
        low, high = LIST_ROWS[part]
        for b, (side, at) in enumerate(blocks):
            src_y = (y_me + OFFSETS[at // N_Z]) & (N_Y - 1)
            src_core = core if side == 0 else 1 - core
            run = runs[(at % N_Z) * 2 * N_Y + src_y * 2 + src_core]
            table[BLOCKS, run] = side * SRC + at
            first = b * 256 + clip_valid(counts, run)
            second = b * 256 + 128 + clip_valid(counts, RUNS - 1 - run)
            table[high, n_high] = first
            n_high = n_high + 1
            table[high, n_high] = second
            n_high = n_high + (run > my_run).astype(jnp.int32)
            table[low, n_low] = first
            n_low = n_low + (run < my_run).astype(jnp.int32)
        for r in range(16):
            table[low, n_low + r] = 0
            table[high, n_high + r] = 0
        table[MISC, AT_COUNT + low] = n_low
        table[MISC, AT_COUNT + high] = n_high
    table[MISC, AT_RUN] = my_run


def lists(runs, counts):
    return pl.pallas_call(
        lists_kernel,
        out_shape=jax.ShapeDtypeStruct((8, LANES), jnp.int32),
        in_specs=[SMEM, SMEM],
        out_specs=SMEM,
        compiler_params=pltpu.CompilerParams(vmem_limit_bytes=BIG_GRANT),
        cost_estimate=pl.CostEstimate(flops=2_000_000, bytes_accessed=300_000, transcendentals=0),
        name="lists",
    )(runs, counts)


AT_PLACE, AT_PICK = 0, 8


def page_of(owner_row, head, me):
    page = jnp.int32(0)
    for p in range(N_CP):
        page = jnp.where(owner_row[head, p] == me, p, page)
    return page


def route_kernel(lists, counts, owner_row, owner_col, owner_slot, table):
    me, z_me, _, _ = coordinates()
    tp = lax.axis_index("tp")
    for i in range(N_X):
        for d in range(2):
            head = i + ((tp & N_X) ^ (d * N_X))
            p = page_of(owner_row, head, me)
            mine = owner_col[head, p] == tp
            table[i * 2 + d] = jnp.where(mine, owner_slot[head, p], -1)

    for k in range(4):
        row = me if k < 2 else me + (N_Z - 1 - 2 * z_me) * 2 * N_Y
        if k % 2 == 0:
            page = page_of(owner_row, tp, row)
        run = page * 2 + k % 2
        second = run >= N_CP
        block = lists[BLOCKS, jnp.where(second, RUNS - 1 - run, run)]
        at = AT_PICK + 4 * k
        table[at] = lax.shift_right_logical(block, 5)
        table[at + 1] = block & (SRC - 1)
        table[at + 2] = second.astype(jnp.int32)
        table[at + 3] = clip_valid(counts, run)


def route(lists, counts, owner_row, owner_col, owner_slot):
    return pl.pallas_call(
        route_kernel,
        out_shape=jax.ShapeDtypeStruct((LANES,), jnp.int32),
        in_specs=[SMEM] * 5,
        out_specs=SMEM,
        compiler_params=pltpu.CompilerParams(vmem_limit_bytes=BIG_GRANT),
        cost_estimate=pl.CostEstimate(flops=2_000_000, bytes_accessed=300_000, transcendentals=0),
        name="route",
    )(lists, counts, owner_row, owner_col, owner_slot)


COLS = KVH * HALF
SCALE = math.log2(math.e) / math.sqrt(HD)
dot = functools.partial(lax.dot_general, preferred_element_type=jnp.float32)


def fold(q, keys, vals, bias, allowed, state):
    top, total, acc = state
    s = dot(keys, q, (((1,), (1,)), ((), ()))) * SCALE
    s = s + jnp.concatenate([bias] * (COLS // HD), axis=1)
    if allowed is not None:
        s = jnp.where(allowed, s, -BIG)
    new_top = jnp.maximum(top, jnp.max(s, axis=0, keepdims=True))
    factor = jnp.exp2(top - new_top)
    w = jnp.exp2(s - new_top)
    total = total * factor + jnp.sum(w, axis=0, keepdims=True)
    acc = acc * factor + dot(vals, w.astype(jnp.bfloat16), (((0,), (0,)), ((), ())))
    return new_top, total, acc


def bias_of(valid):
    return jnp.where(lax.broadcasted_iota(jnp.int32, (HALF, HD), 0) < valid, 0.0, -BIG)


def fold_list(table, row, q, kv, state):
    def chunk(size, start, state):
        ks, vs, biases = [], [], []
        for r in range(size):
            code = table[row, start + r]
            b = lax.shift_right_logical(code, 8)
            rows = pl.ds(pl.multiple_of(lax.shift_right_logical(code & 128, 1), HALF), HALF)
            ks.append(kv[b, 0, rows, :])
            vs.append(kv[b, 1, rows, :])
            biases.append(bias_of(code & 127))
        return fold(
            q,
            jnp.concatenate(ks, axis=0),
            jnp.concatenate(vs, axis=0),
            jnp.concatenate(biases, axis=0),
            None,
            state,
        )

    count = table[MISC, AT_COUNT + row]
    wide = lax.shift_right_logical(count + 7, 4)
    state = lax.fori_loop(0, wide, lambda i, st: chunk(16, i * 16, st), state)
    narrow = (count > wide * 16).astype(jnp.int32)
    return lax.fori_loop(0, narrow, lambda i, st: chunk(8, wide * 16, st), state)


def copy_blocks(pieces, kv, sems):
    copies, at = [], 0
    for i, (piece, start, size) in enumerate(pieces):
        copies.append(
            pltpu.make_async_copy(
                piece.at[pl.ds(start, size)], kv.at[pl.ds(at, size)], sems.at[i]
            )
        )
        at += size
    for copy in copies:
        copy.start()
    for copy in copies:
        copy.wait()


def first_kernel(table, counts, q_rot, early, f3, b3, tops, totals, accs, kv, sems):
    copy_blocks(((early, 0, EARLY), (f3, 0, N_Z), (b3, 0, N_Z)), kv, sems)
    _, z_me, _, _ = coordinates()
    my_run = table[MISC, AT_RUN]
    key = lax.broadcasted_iota(jnp.int32, (HALF, COLS), 0)
    row = lax.broadcasted_iota(jnp.int32, (HALF, COLS), 1) & (HALF - 1)
    for part in range(2):
        q = q_rot[part]
        state = (
            jnp.full((1, COLS), -BIG, jnp.float32),
            jnp.zeros((1, COLS), jnp.float32),
            jnp.zeros((HD, COLS), jnp.float32),
        )
        run = my_run if part == 0 else RUNS - 1 - my_run
        page = lax.shift_right_logical(run, 1)
        valid = jnp.clip(counts[page] - (run & 1) * HALF, 0, HALF)
        rows = slice(part * HALF, (part + 1) * HALF)
        state = fold(q, kv[z_me, 0, rows], kv[z_me, 1, rows], bias_of(valid), key <= row, state)
        state = fold_list(table, LIST_ROWS[0][part], q, kv, state)
        tops[part], totals[part], accs[part] = state


STATE = (
    jax.ShapeDtypeStruct((2, 1, COLS), jnp.float32),
    jax.ShapeDtypeStruct((2, 1, COLS), jnp.float32),
    jax.ShapeDtypeStruct((2, HD, COLS), jnp.float32),
)


def attend_first(table, counts, q_rot, early, f3, b3):
    return pl.pallas_call(
        first_kernel,
        out_shape=STATE,
        in_specs=[SMEM, SMEM, VMEM, ANY, ANY, ANY],
        out_specs=(VMEM, VMEM, VMEM),
        scratch_shapes=[
            pltpu.VMEM((FIRST, 2, ROWS, HD), jnp.bfloat16),
            pltpu.SemaphoreType.DMA((3,)),
        ],
        compiler_params=pltpu.CompilerParams(vmem_limit_bytes=BIG_GRANT),
        cost_estimate=pl.CostEstimate(
            flops=6_000_000_000, bytes_accessed=3_000_000, transcendentals=2_000_000
        ),
        name="attend_first",
    )(table, counts, q_rot, early, f3, b3)


def middle_kernel(table, q_rot, tops, totals, accs, other, new_tops, new_totals, new_accs, kv, sem):
    copy = pltpu.make_async_copy(other.at[pl.ds(0, MIDDLE)], kv, sem)
    copy.start()
    copy.wait()
    for part in range(2):
        state = tops[part], totals[part], accs[part]
        state = fold_list(table, LIST_ROWS[1][part], q_rot[part], kv, state)
        new_tops[part], new_totals[part], new_accs[part] = state


def attend_middle(table, q_rot, state, other):
    return pl.pallas_call(
        middle_kernel,
        out_shape=STATE,
        in_specs=[SMEM, VMEM, VMEM, VMEM, VMEM, ANY],
        out_specs=(VMEM, VMEM, VMEM),
        scratch_shapes=[
            pltpu.VMEM((MIDDLE, 2, ROWS, HD), jnp.bfloat16),
            pltpu.SemaphoreType.DMA,
        ],
        compiler_params=pltpu.CompilerParams(vmem_limit_bytes=BIG_GRANT),
        cost_estimate=pl.CostEstimate(
            flops=2_000_000_000, bytes_accessed=2_000_000, transcendentals=1_000_000
        ),
        name="attend_middle",
    )(table, q_rot, *state, other)


def rest_kernel(table, q_rot, tops, totals, accs, f4, early, late, out, kv, sems):
    copy_blocks(((f4, 0, N_Z), (early, MIDDLE, EARLY - MIDDLE), (late, 0, LATE)), kv, sems)
    for part in range(2):
        state = tops[part], totals[part], accs[part]
        _, total, acc = fold_list(table, LIST_ROWS[2][part], q_rot[part], kv, state)
        res = jnp.transpose(acc / total).astype(jnp.bfloat16)
        for h in range(KVH):
            out[part * HALF : (part + 1) * HALF, h * HD : (h + 1) * HD] = res[
                h * HALF : (h + 1) * HALF
            ]


def attend_rest(table, q_rot, state, f4, early, late):
    return pl.pallas_call(
        rest_kernel,
        out_shape=jax.ShapeDtypeStruct((ROWS, KVH * HD), jnp.bfloat16),
        in_specs=[SMEM, VMEM, VMEM, VMEM, VMEM, ANY, ANY, ANY],
        out_specs=VMEM,
        scratch_shapes=[
            pltpu.VMEM((REST, 2, ROWS, HD), jnp.bfloat16),
            pltpu.SemaphoreType.DMA((3,)),
        ],
        compiler_params=pltpu.CompilerParams(vmem_limit_bytes=BIG_GRANT),
        cost_estimate=pl.CostEstimate(
            flops=8_000_000_000, bytes_accessed=4_000_000, transcendentals=2_000_000
        ),
        name="attend_rest",
    )(table, q_rot, *state, f4, early, late)


def pick_kernel(table, own_early, own_late, other_early, other_late, mine, sent, held, sems):
    for k in range(4):
        at = AT_PICK + 4 * k
        side, index, second = (table[at + i] for i in range(3))
        rows = pl.ds(pl.multiple_of(second * HALF, HALF), HALF)
        for is_other, early, late in ((0, own_early, own_late), (1, other_early, other_late)):

            @pl.when((side == is_other) & (index < EARLY))
            def _(early=early, k=k, index=index, rows=rows):
                pltpu.make_async_copy(early.at[index, :, rows], held.at[k], sems.at[k]).start()

            @pl.when((side == is_other) & (index >= EARLY))
            def _(late=late, k=k, index=index, rows=rows):
                pltpu.make_async_copy(
                    late.at[index - EARLY, :, rows], held.at[k], sems.at[k]
                ).start()

    row = lax.broadcasted_iota(jnp.int32, (HALF, HD), 0)
    for k in range(4):
        pltpu.make_async_copy(own_late.at[0, :, pl.ds(0, HALF)], held.at[k], sems.at[k]).wait()
        keep = row < table[AT_PICK + 4 * k + 3]
        out = mine if k < 2 else sent
        rows = slice(k % 2 * HALF, (k % 2 + 1) * HALF)
        for i in range(2):
            out[i, rows, :] = jnp.where(keep, held[k, i].astype(jnp.float32), 0.0).astype(
                jnp.bfloat16
            )


def pick(table, own_early, own_late, other_early, other_late):
    page = jax.ShapeDtypeStruct((2, PAGE, HD), jnp.bfloat16)
    return pl.pallas_call(
        pick_kernel,
        out_shape=(page, page),
        in_specs=[SMEM, ANY, ANY, ANY, ANY],
        out_specs=(VMEM, VMEM),
        scratch_shapes=[
            pltpu.VMEM((4, 2, HALF, HD), jnp.bfloat16),
            pltpu.SemaphoreType.DMA((4,)),
        ],
        compiler_params=pltpu.CompilerParams(vmem_limit_bytes=BIG_GRANT),
        cost_estimate=pl.CostEstimate(flops=100_000, bytes_accessed=300_000, transcendentals=0),
        name="pick",
    )(table, own_early, own_late, other_early, other_late)


def place_kernel(table, pages, pool_k, pool_v, sems):
    for slot in range(2):
        empty = True
        for i in range(N_X):
            for hi in range(2):
                hit = table[i * 2 + hi] == slot
                empty = jnp.logical_and(empty, jnp.logical_not(hit))

                @pl.when(hit)
                def _(i=i, hi=hi, slot=slot):
                    pltpu.make_async_copy(pages.at[i, hi, 0], pool_k.at[slot], sems.at[slot, 0]).start()
                    pltpu.make_async_copy(pages.at[i, hi, 1], pool_v.at[slot], sems.at[slot, 1]).start()

        @pl.when(empty)
        def _(slot=slot):
            pool_k[slot] = jnp.zeros((PAGE, HD), jnp.bfloat16)
            pool_v[slot] = jnp.zeros((PAGE, HD), jnp.bfloat16)

        @pl.when(jnp.logical_not(empty))
        def _(slot=slot):
            pltpu.make_async_copy(pages.at[0, 0, 0], pool_k.at[slot], sems.at[slot, 0]).wait()
            pltpu.make_async_copy(pages.at[0, 0, 1], pool_v.at[slot], sems.at[slot, 1]).wait()


def place(table, pages):
    shape = jax.ShapeDtypeStruct((2, PAGE, HD), jnp.bfloat16)
    return pl.pallas_call(
        place_kernel,
        out_shape=(shape, shape),
        in_specs=[SMEM, ANY],
        out_specs=(VMEM, VMEM),
        scratch_shapes=[pltpu.SemaphoreType.DMA((2, 2))],
        compiler_params=pltpu.CompilerParams(vmem_limit_bytes=BIG_GRANT),
        cost_estimate=pl.CostEstimate(flops=100_000, bytes_accessed=800_000, transcendentals=0),
        name="place",
    )(table, pages)


def shards(queries, keys, values, positions, counts, owner_row, owner_col, owner_slot):
    tie = lax.optimization_barrier
    spread = pack(positions, keys, values)
    spread, later_positions = tie((spread, positions))
    unit = lax.all_to_all(spread, "cp", 0, 0, axis_index_groups=Z_GROUPS)
    unit, q_rot, runs = tie((unit, *turn(later_positions, queries)))

    ahead, back = y_pairs(1), y_pairs(-1)
    f1 = lax.ppermute(unit, "cp", ahead)
    b1 = lax.ppermute(unit, "cp", back)
    f1, table = tie((f1, lists(runs, counts)))
    f2 = lax.ppermute(f1, "cp", ahead)
    b2 = lax.ppermute(b1, "cp", back)
    f3 = lax.ppermute(f2, "cp", ahead)
    b3 = lax.ppermute(b2, "cp", back)
    own_early = jnp.concatenate([unit, f1, b1, f2, b2], axis=0)
    other_early = lax.ppermute(own_early, "cp", CORE_PAIRS)
    f3, owner_row = tie((f3, owner_row))
    f4 = lax.ppermute(f3, "cp", ahead)
    state = attend_first(table, counts, q_rot, own_early, f3, b3)
    routes = route(table, counts, owner_row, owner_col, owner_slot)
    f4, state, routes = tie((f4, state, routes))
    own_late = jnp.concatenate([f3, b3, f4], axis=0)
    other_late = lax.ppermute(own_late, "cp", CORE_PAIRS)
    other_late, state = tie((other_late, attend_middle(table, q_rot, state, other_early)))

    mine, sent = pick(routes, own_early, own_late, other_early, other_late)
    across = lax.ppermute(sent, ("cp", "tp"), MIRROR_PAIRS)
    attended = attend_rest(table, q_rot, state, f4, other_early, other_late)
    across, attended = tie((across, attended))
    near = jnp.broadcast_to(jnp.stack([mine, across]), (N_X, 2, 2, PAGE, HD))
    pages = lax.all_to_all(near, "tp", 0, 0, axis_index_groups=X_GROUPS)
    pool_keys, pool_values = place(routes, pages)
    return attended, pool_keys, pool_values


def solution(mesh):
    return jax.shard_map(
        shards,
        mesh=mesh,
        in_specs=(P("cp", "tp"), P("cp", "tp"), P("cp", "tp"), P(), P(), P(), P(), P()),
        out_specs=(P("cp", "tp"), P(("cp", "tp"), None, None), P(("cp", "tp"), None, None)),
        check_vma=False,
    )
```

```python
import functools
import math

import jax
import jax.numpy as jnp
import numpy as np
from jax import lax
from jax.experimental import pallas as pl
from jax.experimental.pallas import tpu as pltpu
from jax.sharding import PartitionSpec as P

KVH = 8
HD = 128
PAGE = 128
HALF = 64
ROWS = 128
N_CP = 64
N_Z = 4
N_Y = 8
N_TP = 8
N_X = 4
SRC = N_CP // 2
LANES = 128
RUNS = 2 * N_CP
BIG = 1e30

THETA = 500000.0
RATES = THETA ** (-np.arange(HALF) * 2.0 / HD)


def cos_sin(positions):
    angles = np.asarray(positions)[:, None] * np.concatenate([RATES, RATES])[None, :]
    return np.stack([np.cos(angles), np.sin(angles)]).astype(np.float32)


RUN_TABLE = cos_sin(np.arange(RUNS) * HALF)
STEP_TABLE = cos_sin(np.arange(HALF))


OFFSETS = (0, -1, 1, -2, 2, -3, 3, 4)
FIRST = 28
MIDDLE = SRC - FIRST
REST = SRC
BIG_GRANT = 24 * 2**20


def cp_index(z, y, core):
    return ((z % N_Z) * N_Y + y % N_Y) * 2 + core


def y_pairs(step):
    return [
        (cp_index(z, y, c), cp_index(z, y + step, c))
        for z in range(N_Z)
        for y in range(N_Y)
        for c in range(2)
    ]


Z_GROUPS = [[cp_index(z, y, c) for z in range(N_Z)] for y in range(N_Y) for c in range(2)]
X_GROUPS = [[hi * N_X + x for x in range(N_X)] for hi in range(2)]
CORE_PAIRS = [(i, i ^ 1) for i in range(N_CP)]
MIRROR_PAIRS = [
    (cp_index(z, y, c) * N_TP + tp, cp_index(N_Z - 1 - z, y, c) * N_TP + (tp ^ N_X))
    for z in range(N_Z)
    for y in range(N_Y)
    for c in range(2)
    for tp in range(N_TP)
]


def angles_of(run_table, step_table, first_run):
    low = lax.broadcasted_iota(jnp.int32, (HALF, HD), 1) < HALF
    cos, sin = [], []
    for run in (first_run, RUNS - 1 - first_run):
        run_cos, run_sin = run_table[0, pl.ds(run, 1), :], run_table[1, pl.ds(run, 1), :]
        cos.append(run_cos * step_table[0] - run_sin * step_table[1])
        part = run_sin * step_table[0] + run_cos * step_table[1]
        sin.append(jnp.where(low, -part, part))
    return jnp.concatenate(cos, axis=0), jnp.concatenate(sin, axis=0)


def turned(x, cos, sin):
    return x * cos + pltpu.roll(x, HALF, 1) * sin


SMEM = pl.BlockSpec(memory_space=pltpu.SMEM)
VMEM = pl.BlockSpec(memory_space=pltpu.VMEM)
ANY = pl.BlockSpec(memory_space=pl.ANY)


def coordinates():
    me = lax.axis_index("cp")
    return me, lax.div(me, 2 * N_Y), lax.rem(lax.div(me, 2), N_Y), lax.rem(me, 2)


def pack_kernel(positions, keys, values, run_table, step_table, out):
    first = lax.shift_right_logical(positions[lax.axis_index("cp") & 7, 0], 6)
    cos, sin = angles_of(run_table, step_table, first)
    k_rot = turned(keys[...].astype(jnp.float32), cos, sin).astype(jnp.bfloat16)
    v = values[...]
    for i in range(N_Z):
        out[i, 0] = k_rot
        out[i, 1] = v


def pack(positions, keys, values):
    def whole(*shape):
        return pl.BlockSpec(shape, lambda i: (0,) * len(shape))

    return pl.pallas_call(
        pack_kernel,
        grid=(1,),
        out_shape=jax.ShapeDtypeStruct((N_Z, 2, ROWS, HD), jnp.bfloat16),
        in_specs=[
            pl.BlockSpec(
                (8, ROWS),
                lambda i: (lax.div(lax.axis_index("cp"), 8), 0),
                memory_space=pltpu.SMEM,
            ),
            whole(ROWS, HD),
            whole(ROWS, HD),
            whole(2, RUNS, HD),
            whole(2, HALF, HD),
        ],
        out_specs=whole(N_Z, 2, ROWS, HD),
        cost_estimate=pl.CostEstimate(flops=1_000_000, bytes_accessed=400_000, transcendentals=0),
        name="pack",
    )(positions.reshape(N_CP, ROWS), keys, values, jnp.asarray(RUN_TABLE), jnp.asarray(STEP_TABLE))


def turn_kernel(positions, queries, run_table, step_table, q_rot, runs):
    for s in range(N_CP):
        runs[s] = lax.shift_right_logical(positions[s * ROWS], 6)
    my_run = runs[lax.axis_index("cp")]
    cos, sin = angles_of(run_table, step_table, my_run)
    for h in range(KVH):
        q = turned(queries[:, h * HD : (h + 1) * HD].astype(jnp.float32), cos, sin)
        q = q.astype(jnp.bfloat16)
        q_rot[0, h * HALF : (h + 1) * HALF, :] = q[:HALF]
        q_rot[1, h * HALF : (h + 1) * HALF, :] = q[HALF:]


def turn(positions, queries):
    return pl.pallas_call(
        turn_kernel,
        out_shape=(
            jax.ShapeDtypeStruct((2, KVH * HALF, HD), jnp.bfloat16),
            jax.ShapeDtypeStruct((N_CP,), jnp.int32),
        ),
        in_specs=[SMEM, VMEM, VMEM, VMEM],
        out_specs=(VMEM, SMEM),
        compiler_params=pltpu.CompilerParams(vmem_limit_bytes=BIG_GRANT),
        cost_estimate=pl.CostEstimate(flops=2_000_000, bytes_accessed=600_000, transcendentals=0),
        name="turn",
    )(positions, queries, jnp.asarray(RUN_TABLE), jnp.asarray(STEP_TABLE))


LIST_ROWS = ((0, 1), (2, 3), (4, 5))
MISC = 6
AT_COUNT, AT_RUN = 0, 8
BLOCKS = 7


def clip_valid(counts, run):
    return jnp.clip(counts[lax.shift_right_logical(run, 1)] - (run & 1) * HALF, 0, HALF)


def lists_kernel(runs, counts, table):
    me, _, y_me, core = coordinates()
    my_run = runs[me]

    for part in range(3):
        side = part // 2
        start, stop = ((0, FIRST), (FIRST, SRC), (0, SRC))[part]
        n_low, n_high = jnp.int32(0), jnp.int32(0)
        low, high = LIST_ROWS[part]
        for b, at in enumerate(range(start, stop)):
            src_y = (y_me + OFFSETS[at // N_Z]) & (N_Y - 1)
            src_core = core if side == 0 else 1 - core
            run = runs[(at % N_Z) * 2 * N_Y + src_y * 2 + src_core]
            table[BLOCKS, run] = side * SRC + at
            first = b * 256 + clip_valid(counts, run)
            second = b * 256 + 128 + clip_valid(counts, RUNS - 1 - run)
            table[high, n_high] = first
            n_high = n_high + 1
            table[high, n_high] = second
            n_high = n_high + (run > my_run).astype(jnp.int32)
            table[low, n_low] = first
            n_low = n_low + (run < my_run).astype(jnp.int32)
        for r in range(16):
            table[low, n_low + r] = 0
            table[high, n_high + r] = 0
        table[MISC, AT_COUNT + low] = n_low
        table[MISC, AT_COUNT + high] = n_high
    table[MISC, AT_RUN] = my_run


def lists(runs, counts):
    return pl.pallas_call(
        lists_kernel,
        out_shape=jax.ShapeDtypeStruct((8, LANES), jnp.int32),
        in_specs=[SMEM, SMEM],
        out_specs=SMEM,
        compiler_params=pltpu.CompilerParams(vmem_limit_bytes=BIG_GRANT),
        cost_estimate=pl.CostEstimate(flops=2_000_000, bytes_accessed=300_000, transcendentals=0),
        name="lists",
    )(runs, counts)


AT_PLACE, AT_PICK = 0, 8


def page_of(owner_row, head, me):
    page = jnp.int32(0)
    for p in range(N_CP):
        page = jnp.where(owner_row[head, p] == me, p, page)
    return page


def route_kernel(lists, counts, owner_row, owner_col, owner_slot, table):
    me, z_me, _, _ = coordinates()
    tp = lax.axis_index("tp")
    for i in range(N_X):
        for d in range(2):
            head = i + ((tp & N_X) ^ (d * N_X))
            p = page_of(owner_row, head, me)
            mine = owner_col[head, p] == tp
            table[i * 2 + d] = jnp.where(mine, owner_slot[head, p], -1)

    for k in range(8):
        row = me if k < 4 else me ^ 1
        if k // 2 % 2 == 1:
            row = row + (N_Z - 1 - 2 * z_me) * 2 * N_Y
        if k % 2 == 0:
            page = page_of(owner_row, tp, row)
        run = page * 2 + k % 2
        second = run >= N_CP
        block = lists[BLOCKS, jnp.where(second, RUNS - 1 - run, run)]
        at = AT_PICK + 3 * k
        table[at] = block & (SRC - 1)
        table[at + 1] = second.astype(jnp.int32)
        table[at + 2] = jnp.where(block < SRC, clip_valid(counts, run), 0)


def route(lists, counts, owner_row, owner_col, owner_slot):
    return pl.pallas_call(
        route_kernel,
        out_shape=jax.ShapeDtypeStruct((LANES,), jnp.int32),
        in_specs=[SMEM] * 5,
        out_specs=SMEM,
        compiler_params=pltpu.CompilerParams(vmem_limit_bytes=BIG_GRANT),
        cost_estimate=pl.CostEstimate(flops=2_000_000, bytes_accessed=300_000, transcendentals=0),
        name="route",
    )(lists, counts, owner_row, owner_col, owner_slot)


COLS = KVH * HALF
SCALE = math.log2(math.e) / math.sqrt(HD)
dot = functools.partial(lax.dot_general, preferred_element_type=jnp.float32)


def fold(q, keys, vals, bias, allowed, state):
    top, total, acc = state
    s = dot(keys, q, (((1,), (1,)), ((), ()))) * SCALE
    s = s + jnp.concatenate([bias] * (COLS // HD), axis=1)
    if allowed is not None:
        s = jnp.where(allowed, s, -BIG)
    new_top = jnp.maximum(top, jnp.max(s, axis=0, keepdims=True))
    factor = jnp.exp2(top - new_top)
    w = jnp.exp2(s - new_top)
    total = total * factor + jnp.sum(w, axis=0, keepdims=True)
    acc = acc * factor + dot(vals, w.astype(jnp.bfloat16), (((0,), (0,)), ((), ())))
    return new_top, total, acc


def bias_of(valid):
    return jnp.where(lax.broadcasted_iota(jnp.int32, (HALF, HD), 0) < valid, 0.0, -BIG)


def fold_list(table, row, q, kv, state):
    def chunk(size, start, state):
        ks, vs, biases = [], [], []
        for r in range(size):
            code = table[row, start + r]
            b = lax.shift_right_logical(code, 8)
            rows = pl.ds(pl.multiple_of(lax.shift_right_logical(code & 128, 1), HALF), HALF)
            ks.append(kv[b, 0, rows, :])
            vs.append(kv[b, 1, rows, :])
            biases.append(bias_of(code & 127))
        return fold(
            q,
            jnp.concatenate(ks, axis=0),
            jnp.concatenate(vs, axis=0),
            jnp.concatenate(biases, axis=0),
            None,
            state,
        )

    count = table[MISC, AT_COUNT + row]
    wide = lax.shift_right_logical(count + 7, 4)
    state = lax.fori_loop(0, wide, lambda i, st: chunk(16, i * 16, st), state)
    narrow = (count > wide * 16).astype(jnp.int32)
    return lax.fori_loop(0, narrow, lambda i, st: chunk(8, wide * 16, st), state)


def copy_blocks(pieces, kv, sems):
    copies, at = [], 0
    for i, (piece, start, size) in enumerate(pieces):
        copies.append(
            pltpu.make_async_copy(
                piece.at[pl.ds(start, size)], kv.at[pl.ds(at, size)], sems.at[i]
            )
        )
        at += size
    for copy in copies:
        copy.start()
    for copy in copies:
        copy.wait()


def first_kernel(table, counts, q_rot, *refs):
    pieces, (tops, totals, accs, kv, sems) = refs[:-5], refs[-5:]
    copy_blocks([(piece, 0, N_Z) for piece in pieces], kv, sems)
    _, z_me, _, _ = coordinates()
    my_run = table[MISC, AT_RUN]
    key = lax.broadcasted_iota(jnp.int32, (HALF, COLS), 0)
    row = lax.broadcasted_iota(jnp.int32, (HALF, COLS), 1) & (HALF - 1)
    for part in range(2):
        q = q_rot[part]
        state = (
            jnp.full((1, COLS), -BIG, jnp.float32),
            jnp.zeros((1, COLS), jnp.float32),
            jnp.zeros((HD, COLS), jnp.float32),
        )
        run = my_run if part == 0 else RUNS - 1 - my_run
        page = lax.shift_right_logical(run, 1)
        valid = jnp.clip(counts[page] - (run & 1) * HALF, 0, HALF)
        rows = slice(part * HALF, (part + 1) * HALF)
        state = fold(q, kv[z_me, 0, rows], kv[z_me, 1, rows], bias_of(valid), key <= row, state)
        state = fold_list(table, LIST_ROWS[0][part], q, kv, state)
        tops[part], totals[part], accs[part] = state


STATE = (
    jax.ShapeDtypeStruct((2, 1, COLS), jnp.float32),
    jax.ShapeDtypeStruct((2, 1, COLS), jnp.float32),
    jax.ShapeDtypeStruct((2, HD, COLS), jnp.float32),
)


def attend_first(table, counts, q_rot, *pieces):
    return pl.pallas_call(
        first_kernel,
        out_shape=STATE,
        in_specs=[SMEM, SMEM, VMEM] + [ANY] * len(pieces),
        out_specs=(VMEM, VMEM, VMEM),
        scratch_shapes=[
            pltpu.VMEM((FIRST, 2, ROWS, HD), jnp.bfloat16),
            pltpu.SemaphoreType.DMA((len(pieces),)),
        ],
        compiler_params=pltpu.CompilerParams(vmem_limit_bytes=BIG_GRANT),
        cost_estimate=pl.CostEstimate(
            flops=6_000_000_000, bytes_accessed=3_000_000, transcendentals=2_000_000
        ),
        name="attend_first",
    )(table, counts, q_rot, *pieces)


def middle_kernel(table, q_rot, tops, totals, accs, other, new_tops, new_totals, new_accs, kv, sem):
    copy = pltpu.make_async_copy(other, kv, sem)
    copy.start()
    copy.wait()
    for part in range(2):
        state = tops[part], totals[part], accs[part]
        state = fold_list(table, LIST_ROWS[1][part], q_rot[part], kv, state)
        new_tops[part], new_totals[part], new_accs[part] = state


def attend_middle(table, q_rot, state, other):
    return pl.pallas_call(
        middle_kernel,
        out_shape=STATE,
        in_specs=[SMEM, VMEM, VMEM, VMEM, VMEM, ANY],
        out_specs=(VMEM, VMEM, VMEM),
        scratch_shapes=[
            pltpu.VMEM((MIDDLE, 2, ROWS, HD), jnp.bfloat16),
            pltpu.SemaphoreType.DMA,
        ],
        compiler_params=pltpu.CompilerParams(vmem_limit_bytes=BIG_GRANT),
        cost_estimate=pl.CostEstimate(
            flops=2_000_000_000, bytes_accessed=2_000_000, transcendentals=1_000_000
        ),
        name="attend_middle",
    )(table, q_rot, *state, other)


def rest_kernel(table, q_rot, tops, totals, accs, other, out, kv, sem):
    copy = pltpu.make_async_copy(other, kv, sem)
    copy.start()
    copy.wait()
    for part in range(2):
        state = tops[part], totals[part], accs[part]
        _, total, acc = fold_list(table, LIST_ROWS[2][part], q_rot[part], kv, state)
        res = jnp.transpose(acc / total).astype(jnp.bfloat16)
        for h in range(KVH):
            out[part * HALF : (part + 1) * HALF, h * HD : (h + 1) * HD] = res[
                h * HALF : (h + 1) * HALF
            ]


def attend_rest(table, q_rot, state, other):
    return pl.pallas_call(
        rest_kernel,
        out_shape=jax.ShapeDtypeStruct((ROWS, KVH * HD), jnp.bfloat16),
        in_specs=[SMEM, VMEM, VMEM, VMEM, VMEM, ANY],
        out_specs=VMEM,
        scratch_shapes=[
            pltpu.VMEM((REST, 2, ROWS, HD), jnp.bfloat16),
            pltpu.SemaphoreType.DMA,
        ],
        compiler_params=pltpu.CompilerParams(vmem_limit_bytes=BIG_GRANT),
        cost_estimate=pl.CostEstimate(
            flops=8_000_000_000, bytes_accessed=4_000_000, transcendentals=2_000_000
        ),
        name="attend_rest",
    )(table, q_rot, *state, other)


def pick_kernel(table, own, mine, theirs, held, sems):
    copies = []
    for k in range(8):
        index, second = table[AT_PICK + 3 * k], table[AT_PICK + 3 * k + 1]
        rows = pl.ds(pl.multiple_of(second * HALF, HALF), HALF)
        copies.append(pltpu.make_async_copy(own.at[index, :, rows], held.at[k], sems.at[k]))
        copies[-1].start()
    row = lax.broadcasted_iota(jnp.int32, (HALF, HD), 0)
    for k in range(8):
        copies[k].wait()
        keep = row < table[AT_PICK + 3 * k + 2]
        out = mine if k < 4 else theirs
        rows = slice(k % 2 * HALF, (k % 2 + 1) * HALF)
        for i in range(2):
            out[k // 2 % 2, i, rows, :] = jnp.where(
                keep, held[k, i].astype(jnp.float32), 0.0
            ).astype(jnp.bfloat16)


def pick(table, own):
    pages = jax.ShapeDtypeStruct((2, 2, PAGE, HD), jnp.bfloat16)
    return pl.pallas_call(
        pick_kernel,
        out_shape=(pages, pages),
        in_specs=[SMEM, ANY],
        out_specs=(VMEM, VMEM),
        scratch_shapes=[
            pltpu.VMEM((8, 2, HALF, HD), jnp.bfloat16),
            pltpu.SemaphoreType.DMA((8,)),
        ],
        compiler_params=pltpu.CompilerParams(vmem_limit_bytes=BIG_GRANT),
        cost_estimate=pl.CostEstimate(flops=100_000, bytes_accessed=300_000, transcendentals=0),
        name="pick",
    )(table, own)


def spread_kernel(mine, across, out):
    for i in range(N_X):
        out[i, 0] = mine[0]
        out[i, 1] = across[...]


def spread(mine, across):
    return pl.pallas_call(
        spread_kernel,
        out_shape=jax.ShapeDtypeStruct((N_X, 2, 2, PAGE, HD), jnp.bfloat16),
        in_specs=[VMEM, VMEM],
        out_specs=VMEM,
        cost_estimate=pl.CostEstimate(
            flops=100_000_000_000, bytes_accessed=700_000, transcendentals=0
        ),
        name="spread",
    )(mine, across)


def place_kernel(table, pages, pool_k, pool_v, sems):
    for slot in range(2):
        empty = True
        for i in range(N_X):
            for hi in range(2):
                hit = table[i * 2 + hi] == slot
                empty = jnp.logical_and(empty, jnp.logical_not(hit))

                @pl.when(hit)
                def _(i=i, hi=hi, slot=slot):
                    pltpu.make_async_copy(pages.at[i, hi, 0], pool_k.at[slot], sems.at[slot, 0]).start()
                    pltpu.make_async_copy(pages.at[i, hi, 1], pool_v.at[slot], sems.at[slot, 1]).start()

        @pl.when(empty)
        def _(slot=slot):
            pool_k[slot] = jnp.zeros((PAGE, HD), jnp.bfloat16)
            pool_v[slot] = jnp.zeros((PAGE, HD), jnp.bfloat16)

        @pl.when(jnp.logical_not(empty))
        def _(slot=slot):
            pltpu.make_async_copy(pages.at[0, 0, 0], pool_k.at[slot], sems.at[slot, 0]).wait()
            pltpu.make_async_copy(pages.at[0, 0, 1], pool_v.at[slot], sems.at[slot, 1]).wait()


def place(table, pages):
    shape = jax.ShapeDtypeStruct((2, PAGE, HD), jnp.bfloat16)
    return pl.pallas_call(
        place_kernel,
        out_shape=(shape, shape),
        in_specs=[SMEM, ANY],
        out_specs=(VMEM, VMEM),
        scratch_shapes=[pltpu.SemaphoreType.DMA((2, 2))],
        compiler_params=pltpu.CompilerParams(vmem_limit_bytes=BIG_GRANT),
        cost_estimate=pl.CostEstimate(flops=100_000, bytes_accessed=800_000, transcendentals=0),
        name="place",
    )(table, pages)


def shards(queries, keys, values, positions, counts, owner_row, owner_col, owner_slot):
    tie = lax.optimization_barrier
    packed, later_positions = tie((pack(positions, keys, values), positions))
    unit = lax.all_to_all(packed, "cp", 0, 0, axis_index_groups=Z_GROUPS)
    unit, q_rot, runs = tie((unit, *turn(later_positions, queries)))

    ahead, back = y_pairs(1), y_pairs(-1)
    f1 = lax.ppermute(unit, "cp", ahead)
    b1 = lax.ppermute(unit, "cp", back)
    f1, table = tie((f1, lists(runs, counts)))
    f2 = lax.ppermute(f1, "cp", ahead)
    b2 = lax.ppermute(b1, "cp", back)
    f3 = lax.ppermute(f2, "cp", ahead)
    b3 = lax.ppermute(b2, "cp", back)
    f4 = lax.ppermute(f3, "cp", ahead)
    state = attend_first(table, counts, q_rot, unit, f1, b1, f2, b2, f3, b3)
    routes = route(table, counts, owner_row, owner_col, owner_slot)
    f4, state, routes = tie((f4, state, routes))
    own = jnp.concatenate([unit, f1, b1, f2, b2, f3, b3, f4], axis=0)

    mine, theirs = pick(routes, own)
    pages = mine + lax.ppermute(theirs, "cp", CORE_PAIRS)
    across = lax.ppermute(pages[1], ("cp", "tp"), MIRROR_PAIRS)
    pages, state = tie((pages, state))
    state = attend_middle(table, q_rot, state, f4)
    own, state = tie((own, state))
    other = lax.ppermute(own, "cp", CORE_PAIRS)
    across, state = tie((across, state))
    pages = lax.all_to_all(spread(pages, across), "tp", 0, 0, axis_index_groups=X_GROUPS)
    pages, attended = tie((pages, attend_rest(table, q_rot, state, other)))
    pool_keys, pool_values = place(routes, pages)
    return attended, pool_keys, pool_values


def solution(mesh):
    return jax.shard_map(
        shards,
        mesh=mesh,
        in_specs=(P("cp", "tp"), P("cp", "tp"), P("cp", "tp"), P(), P(), P(), P(), P()),
        out_specs=(P("cp", "tp"), P(("cp", "tp"), None, None), P(("cp", "tp"), None, None)),
        check_vma=False,
    )
```

```python
import functools
import math

import jax
import jax.numpy as jnp
import numpy as np
from jax import lax
from jax.experimental import pallas as pl
from jax.experimental.pallas import tpu as pltpu
from jax.sharding import PartitionSpec as P

KVH = 8
HD = 128
PAGE = 128
HALF = 64
ROWS = 128
N_CP = 64
N_Z = 4
N_Y = 8
N_TP = 8
N_X = 4
SRC = N_CP // 2
LANES = 128
RUNS = 2 * N_CP
BIG = 1e30

THETA = 500000.0
RATES = THETA ** (-np.arange(HALF) * 2.0 / HD)


def cos_sin(positions):
    angles = np.asarray(positions)[:, None] * np.concatenate([RATES, RATES])[None, :]
    return np.stack([np.cos(angles), np.sin(angles)]).astype(np.float32)


RUN_TABLE = cos_sin(np.arange(RUNS) * HALF)
STEP_TABLE = cos_sin(np.arange(HALF))


OFFSETS = (0, -1, 1, -2, 2, -3, 3, 4)
FIRST = 28
MIDDLE = SRC - FIRST
REST = SRC
BIG_GRANT = 24 * 2**20


def cp_index(z, y, core):
    return ((z % N_Z) * N_Y + y % N_Y) * 2 + core


def y_pairs(step):
    return [
        (cp_index(z, y, c), cp_index(z, y + step, c))
        for z in range(N_Z)
        for y in range(N_Y)
        for c in range(2)
    ]


Z_GROUPS = [[cp_index(z, y, c) for z in range(N_Z)] for y in range(N_Y) for c in range(2)]
X_GROUPS = [[hi * N_X + x for x in range(N_X)] for hi in range(2)]
CORE_PAIRS = [(i, i ^ 1) for i in range(N_CP)]
MIRROR_PAIRS = [
    (cp_index(z, y, c) * N_TP + tp, cp_index(N_Z - 1 - z, y, c) * N_TP + (tp ^ N_X))
    for z in range(N_Z)
    for y in range(N_Y)
    for c in range(2)
    for tp in range(N_TP)
]


def angles_of(run_table, step_table, first_run):
    low = lax.broadcasted_iota(jnp.int32, (HALF, HD), 1) < HALF
    cos, sin = [], []
    for run in (first_run, RUNS - 1 - first_run):
        run_cos, run_sin = run_table[0, pl.ds(run, 1), :], run_table[1, pl.ds(run, 1), :]
        cos.append(run_cos * step_table[0] - run_sin * step_table[1])
        part = run_sin * step_table[0] + run_cos * step_table[1]
        sin.append(jnp.where(low, -part, part))
    return jnp.concatenate(cos, axis=0), jnp.concatenate(sin, axis=0)


def turned(x, cos, sin):
    return x * cos + pltpu.roll(x, HALF, 1) * sin


SMEM = pl.BlockSpec(memory_space=pltpu.SMEM)
VMEM = pl.BlockSpec(memory_space=pltpu.VMEM)
ANY = pl.BlockSpec(memory_space=pl.ANY)


def coordinates():
    me = lax.axis_index("cp")
    return me, lax.div(me, 2 * N_Y), lax.rem(lax.div(me, 2), N_Y), lax.rem(me, 2)


def pack_kernel(positions, keys, values, run_table, step_table, out):
    first = lax.shift_right_logical(positions[lax.axis_index("cp") & 7, 0], 6)
    cos, sin = angles_of(run_table, step_table, first)
    k_rot = turned(keys[...].astype(jnp.float32), cos, sin).astype(jnp.bfloat16)
    v = values[...]
    for i in range(N_Z):
        out[i, 0] = k_rot
        out[i, 1] = v


def pack(positions, keys, values):
    def whole(*shape):
        return pl.BlockSpec(shape, lambda i: (0,) * len(shape))

    return pl.pallas_call(
        pack_kernel,
        grid=(1,),
        out_shape=jax.ShapeDtypeStruct((N_Z, 2, ROWS, HD), jnp.bfloat16),
        in_specs=[
            pl.BlockSpec(
                (8, ROWS),
                lambda i: (lax.div(lax.axis_index("cp"), 8), 0),
                memory_space=pltpu.SMEM,
            ),
            whole(ROWS, HD),
            whole(ROWS, HD),
            whole(2, RUNS, HD),
            whole(2, HALF, HD),
        ],
        out_specs=whole(N_Z, 2, ROWS, HD),
        cost_estimate=pl.CostEstimate(flops=1_000_000, bytes_accessed=400_000, transcendentals=0),
        name="pack",
    )(positions.reshape(N_CP, ROWS), keys, values, jnp.asarray(RUN_TABLE), jnp.asarray(STEP_TABLE))


def turn_kernel(positions, queries, run_table, step_table, q_rot, runs):
    for s in range(N_CP):
        runs[s] = lax.shift_right_logical(positions[s * ROWS], 6)
    my_run = runs[lax.axis_index("cp")]
    cos, sin = angles_of(run_table, step_table, my_run)
    for h in range(KVH):
        q = turned(queries[:, h * HD : (h + 1) * HD].astype(jnp.float32), cos, sin)
        q = q.astype(jnp.bfloat16)
        q_rot[0, h * HALF : (h + 1) * HALF, :] = q[:HALF]
        q_rot[1, h * HALF : (h + 1) * HALF, :] = q[HALF:]


def turn(positions, queries):
    return pl.pallas_call(
        turn_kernel,
        out_shape=(
            jax.ShapeDtypeStruct((2, KVH * HALF, HD), jnp.bfloat16),
            jax.ShapeDtypeStruct((N_CP,), jnp.int32),
        ),
        in_specs=[SMEM, VMEM, VMEM, VMEM],
        out_specs=(VMEM, SMEM),
        cost_estimate=pl.CostEstimate(flops=2_000_000, bytes_accessed=600_000, transcendentals=0),
        name="turn",
    )(positions, queries, jnp.asarray(RUN_TABLE), jnp.asarray(STEP_TABLE))


LIST_ROWS = ((0, 1), (2, 3), (4, 5))
MISC = 6
AT_COUNT, AT_RUN = 0, 8
BLOCKS = 7


def clip_valid(counts, run):
    return jnp.clip(counts[lax.shift_right_logical(run, 1)] - (run & 1) * HALF, 0, HALF)


def lists_kernel(runs, counts, owner_row, owner_col, owner_slot, table, routes):
    me, _, y_me, core = coordinates()
    my_run = runs[me]

    for part in range(3):
        side = part // 2
        start, stop = ((0, FIRST), (FIRST, SRC), (0, SRC))[part]
        n_low, n_high = jnp.int32(0), jnp.int32(0)
        low, high = LIST_ROWS[part]
        for b, at in enumerate(range(start, stop)):
            src_y = (y_me + OFFSETS[at // N_Z]) & (N_Y - 1)
            src_core = core if side == 0 else 1 - core
            run = runs[(at % N_Z) * 2 * N_Y + src_y * 2 + src_core]
            table[BLOCKS, run] = side * SRC + at
            first = b * 256 + clip_valid(counts, run)
            second = b * 256 + 128 + clip_valid(counts, RUNS - 1 - run)
            table[high, n_high] = first
            n_high = n_high + 1
            table[high, n_high] = second
            n_high = n_high + (run > my_run).astype(jnp.int32)
            table[low, n_low] = first
            n_low = n_low + (run < my_run).astype(jnp.int32)
        for r in range(16):
            table[low, n_low + r] = 0
            table[high, n_high + r] = 0
        table[MISC, AT_COUNT + low] = n_low
        table[MISC, AT_COUNT + high] = n_high
    table[MISC, AT_RUN] = my_run
    route_entries(table, counts, owner_row, owner_col, owner_slot, routes)


AT_PLACE, AT_PICK = 0, 8


def page_of(owner_row, head, me):
    page = jnp.int32(0)
    for p in range(N_CP):
        page = jnp.where(owner_row[head, p] == me, p, page)
    return page


def route_entries(lists, counts, owner_row, owner_col, owner_slot, table):
    me, z_me, _, _ = coordinates()
    tp = lax.axis_index("tp")
    for i in range(N_X):
        for d in range(2):
            head = i + ((tp & N_X) ^ (d * N_X))
            p = page_of(owner_row, head, me)
            mine = owner_col[head, p] == tp
            table[i * 2 + d] = jnp.where(mine, owner_slot[head, p], -1)

    for k in range(8):
        row = me if k < 4 else me ^ 1
        if k // 2 % 2 == 1:
            row = row + (N_Z - 1 - 2 * z_me) * 2 * N_Y
        if k % 2 == 0:
            page = page_of(owner_row, tp, row)
        run = page * 2 + k % 2
        second = run >= N_CP
        block = lists[BLOCKS, jnp.where(second, RUNS - 1 - run, run)]
        at = AT_PICK + 3 * k
        table[at] = block & (SRC - 1)
        table[at + 1] = second.astype(jnp.int32)
        table[at + 2] = jnp.where(block < SRC, clip_valid(counts, run), 0)


def lists(runs, counts, owner_row, owner_col, owner_slot):
    return pl.pallas_call(
        lists_kernel,
        out_shape=(
            jax.ShapeDtypeStruct((8, LANES), jnp.int32),
            jax.ShapeDtypeStruct((LANES,), jnp.int32),
        ),
        in_specs=[SMEM] * 5,
        out_specs=(SMEM, SMEM),
        cost_estimate=pl.CostEstimate(flops=2_000_000, bytes_accessed=300_000, transcendentals=0),
        name="lists",
    )(runs, counts, owner_row, owner_col, owner_slot)


COLS = KVH * HALF
SCALE = math.log2(math.e) / math.sqrt(HD)
dot = functools.partial(lax.dot_general, preferred_element_type=jnp.float32)


def fold(q, keys, vals, bias, allowed, state):
    top, total, acc = state
    s = dot(keys, q, (((1,), (1,)), ((), ()))) * SCALE
    s = s + jnp.concatenate([bias] * (COLS // HD), axis=1)
    if allowed is not None:
        s = jnp.where(allowed, s, -BIG)
    new_top = jnp.maximum(top, jnp.max(s, axis=0, keepdims=True))
    factor = jnp.exp2(top - new_top)
    w = jnp.exp2(s - new_top)
    total = total * factor + jnp.sum(w, axis=0, keepdims=True)
    acc = acc * factor + dot(vals, w.astype(jnp.bfloat16), (((0,), (0,)), ((), ())))
    return new_top, total, acc


def bias_of(valid):
    return jnp.where(lax.broadcasted_iota(jnp.int32, (HALF, HD), 0) < valid, 0.0, -BIG)


def fold_list(table, row, q, kv, state):
    def chunk(size, start, state):
        ks, vs, biases = [], [], []
        for r in range(size):
            code = table[row, start + r]
            b = lax.shift_right_logical(code, 8)
            rows = pl.ds(pl.multiple_of(lax.shift_right_logical(code & 128, 1), HALF), HALF)
            ks.append(kv[b, 0, rows, :])
            vs.append(kv[b, 1, rows, :])
            biases.append(bias_of(code & 127))
        return fold(
            q,
            jnp.concatenate(ks, axis=0),
            jnp.concatenate(vs, axis=0),
            jnp.concatenate(biases, axis=0),
            None,
            state,
        )

    count = table[MISC, AT_COUNT + row]
    wide = lax.shift_right_logical(count + 7, 4)
    state = lax.fori_loop(0, wide, lambda i, st: chunk(16, i * 16, st), state)
    narrow = (count > wide * 16).astype(jnp.int32)
    return lax.fori_loop(0, narrow, lambda i, st: chunk(8, wide * 16, st), state)


def copy_blocks(pieces, kv, sems):
    copies, at = [], 0
    for i, (piece, start, size) in enumerate(pieces):
        copies.append(
            pltpu.make_async_copy(
                piece.at[pl.ds(start, size)], kv.at[pl.ds(at, size)], sems.at[i]
            )
        )
        at += size
    for copy in copies:
        copy.start()
    for copy in copies:
        copy.wait()


def first_kernel(table, counts, q_rot, *refs):
    pieces, (tops, totals, accs, kv, sems) = refs[:-5], refs[-5:]
    copy_blocks([(piece, 0, N_Z) for piece in pieces], kv, sems)
    _, z_me, _, _ = coordinates()
    my_run = table[MISC, AT_RUN]
    key = lax.broadcasted_iota(jnp.int32, (HALF, COLS), 0)
    row = lax.broadcasted_iota(jnp.int32, (HALF, COLS), 1) & (HALF - 1)
    for part in range(2):
        q = q_rot[part]
        state = (
            jnp.full((1, COLS), -BIG, jnp.float32),
            jnp.zeros((1, COLS), jnp.float32),
            jnp.zeros((HD, COLS), jnp.float32),
        )
        run = my_run if part == 0 else RUNS - 1 - my_run
        page = lax.shift_right_logical(run, 1)
        valid = jnp.clip(counts[page] - (run & 1) * HALF, 0, HALF)
        rows = slice(part * HALF, (part + 1) * HALF)
        state = fold(q, kv[z_me, 0, rows], kv[z_me, 1, rows], bias_of(valid), key <= row, state)
        state = fold_list(table, LIST_ROWS[0][part], q, kv, state)
        tops[part], totals[part], accs[part] = state


STATE = (
    jax.ShapeDtypeStruct((2, 1, COLS), jnp.float32),
    jax.ShapeDtypeStruct((2, 1, COLS), jnp.float32),
    jax.ShapeDtypeStruct((2, HD, COLS), jnp.float32),
)


def attend_first(table, counts, q_rot, *pieces):
    return pl.pallas_call(
        first_kernel,
        out_shape=STATE,
        in_specs=[SMEM, SMEM, VMEM] + [ANY] * len(pieces),
        out_specs=(VMEM, VMEM, VMEM),
        scratch_shapes=[
            pltpu.VMEM((FIRST, 2, ROWS, HD), jnp.bfloat16),
            pltpu.SemaphoreType.DMA((len(pieces),)),
        ],
        compiler_params=pltpu.CompilerParams(vmem_limit_bytes=BIG_GRANT),
        cost_estimate=pl.CostEstimate(
            flops=6_000_000_000, bytes_accessed=3_000_000, transcendentals=2_000_000
        ),
        name="attend_first",
    )(table, counts, q_rot, *pieces)


def middle_kernel(table, q_rot, tops, totals, accs, other, new_tops, new_totals, new_accs, kv, sem):
    copy = pltpu.make_async_copy(other, kv, sem)
    copy.start()
    copy.wait()
    for part in range(2):
        state = tops[part], totals[part], accs[part]
        state = fold_list(table, LIST_ROWS[1][part], q_rot[part], kv, state)
        new_tops[part], new_totals[part], new_accs[part] = state


def attend_middle(table, q_rot, state, other):
    return pl.pallas_call(
        middle_kernel,
        out_shape=STATE,
        in_specs=[SMEM, VMEM, VMEM, VMEM, VMEM, ANY],
        out_specs=(VMEM, VMEM, VMEM),
        scratch_shapes=[
            pltpu.VMEM((MIDDLE, 2, ROWS, HD), jnp.bfloat16),
            pltpu.SemaphoreType.DMA,
        ],
        compiler_params=pltpu.CompilerParams(vmem_limit_bytes=BIG_GRANT),
        cost_estimate=pl.CostEstimate(
            flops=2_000_000_000, bytes_accessed=2_000_000, transcendentals=1_000_000
        ),
        name="attend_middle",
    )(table, q_rot, *state, other)


def rest_kernel(table, q_rot, tops, totals, accs, other, out, kv, sem):
    copy = pltpu.make_async_copy(other, kv, sem)
    copy.start()
    copy.wait()
    for part in range(2):
        state = tops[part], totals[part], accs[part]
        _, total, acc = fold_list(table, LIST_ROWS[2][part], q_rot[part], kv, state)
        res = jnp.transpose(acc / total).astype(jnp.bfloat16)
        for h in range(KVH):
            out[part * HALF : (part + 1) * HALF, h * HD : (h + 1) * HD] = res[
                h * HALF : (h + 1) * HALF
            ]


def attend_rest(table, q_rot, state, other):
    return pl.pallas_call(
        rest_kernel,
        out_shape=jax.ShapeDtypeStruct((ROWS, KVH * HD), jnp.bfloat16),
        in_specs=[SMEM, VMEM, VMEM, VMEM, VMEM, ANY],
        out_specs=VMEM,
        scratch_shapes=[
            pltpu.VMEM((REST, 2, ROWS, HD), jnp.bfloat16),
            pltpu.SemaphoreType.DMA,
        ],
        compiler_params=pltpu.CompilerParams(vmem_limit_bytes=BIG_GRANT),
        cost_estimate=pl.CostEstimate(
            flops=8_000_000_000, bytes_accessed=4_000_000, transcendentals=2_000_000
        ),
        name="attend_rest",
    )(table, q_rot, *state, other)


def pick_kernel(table, own, mine, theirs, held, sems):
    copies = []
    for k in range(8):
        index, second = table[AT_PICK + 3 * k], table[AT_PICK + 3 * k + 1]
        rows = pl.ds(pl.multiple_of(second * HALF, HALF), HALF)
        copies.append(pltpu.make_async_copy(own.at[index, :, rows], held.at[k], sems.at[k]))
        copies[-1].start()
    row = lax.broadcasted_iota(jnp.int32, (HALF, HD), 0)
    for k in range(8):
        copies[k].wait()
        keep = row < table[AT_PICK + 3 * k + 2]
        out = mine if k < 4 else theirs
        rows = slice(k % 2 * HALF, (k % 2 + 1) * HALF)
        for i in range(2):
            out[k // 2 % 2, i, rows, :] = jnp.where(
                keep, held[k, i].astype(jnp.float32), 0.0
            ).astype(jnp.bfloat16)


def pick(table, own):
    pages = jax.ShapeDtypeStruct((2, 2, PAGE, HD), jnp.bfloat16)
    return pl.pallas_call(
        pick_kernel,
        out_shape=(pages, pages),
        in_specs=[SMEM, ANY],
        out_specs=(VMEM, VMEM),
        scratch_shapes=[
            pltpu.VMEM((8, 2, HALF, HD), jnp.bfloat16),
            pltpu.SemaphoreType.DMA((8,)),
        ],
        compiler_params=pltpu.CompilerParams(vmem_limit_bytes=BIG_GRANT),
        cost_estimate=pl.CostEstimate(flops=100_000, bytes_accessed=300_000, transcendentals=0),
        name="pick",
    )(table, own)


def spread_kernel(mine, across, out):
    for i in range(N_X):
        out[i, 0] = mine[0]
        out[i, 1] = across[...]


def spread(mine, across):
    return pl.pallas_call(
        spread_kernel,
        grid=(1,),
        out_shape=jax.ShapeDtypeStruct((N_X, 2, 2, PAGE, HD), jnp.bfloat16),
        in_specs=[
            pl.BlockSpec((1, 2, PAGE, HD), lambda i: (0, 0, 0, 0)),
            pl.BlockSpec((2, PAGE, HD), lambda i: (0, 0, 0)),
        ],
        out_specs=pl.BlockSpec((N_X, 2, 2, PAGE, HD), lambda i: (0, 0, 0, 0, 0)),
        compiler_params=pltpu.CompilerParams(vmem_limit_bytes=BIG_GRANT),
        cost_estimate=pl.CostEstimate(
            flops=100_000_000_000, bytes_accessed=700_000, transcendentals=0
        ),
        name="spread",
    )(mine, across)


def place_kernel(table, pages, pool_k, pool_v, sems):
    for slot in range(2):
        empty = True
        for i in range(N_X):
            for hi in range(2):
                hit = table[i * 2 + hi] == slot
                empty = jnp.logical_and(empty, jnp.logical_not(hit))

                @pl.when(hit)
                def _(i=i, hi=hi, slot=slot):
                    pltpu.make_async_copy(pages.at[i, hi, 0], pool_k.at[slot], sems.at[slot, 0]).start()
                    pltpu.make_async_copy(pages.at[i, hi, 1], pool_v.at[slot], sems.at[slot, 1]).start()

        @pl.when(empty)
        def _(slot=slot):
            pool_k[slot] = jnp.zeros((PAGE, HD), jnp.bfloat16)
            pool_v[slot] = jnp.zeros((PAGE, HD), jnp.bfloat16)

        @pl.when(jnp.logical_not(empty))
        def _(slot=slot):
            pltpu.make_async_copy(pages.at[0, 0, 0], pool_k.at[slot], sems.at[slot, 0]).wait()
            pltpu.make_async_copy(pages.at[0, 0, 1], pool_v.at[slot], sems.at[slot, 1]).wait()


def place(table, pages):
    shape = jax.ShapeDtypeStruct((2, PAGE, HD), jnp.bfloat16)
    return pl.pallas_call(
        place_kernel,
        out_shape=(shape, shape),
        in_specs=[SMEM, ANY],
        out_specs=(VMEM, VMEM),
        scratch_shapes=[pltpu.SemaphoreType.DMA((2, 2))],
        compiler_params=pltpu.CompilerParams(vmem_limit_bytes=BIG_GRANT),
        cost_estimate=pl.CostEstimate(flops=100_000, bytes_accessed=800_000, transcendentals=0),
        name="place",
    )(table, pages)


def shards(queries, keys, values, positions, counts, owner_row, owner_col, owner_slot):
    tie = lax.optimization_barrier
    packed, later_positions = tie((pack(positions, keys, values), positions))
    unit = lax.all_to_all(packed, "cp", 0, 0, axis_index_groups=Z_GROUPS)
    q_rot, runs = turn(later_positions, queries)
    table, routes = lists(runs, counts, owner_row, owner_col, owner_slot)
    unit, q_rot, table, routes = tie((unit, q_rot, table, routes))

    ahead, back = y_pairs(1), y_pairs(-1)
    f1 = lax.ppermute(unit, "cp", ahead)
    b1 = lax.ppermute(unit, "cp", back)
    f2 = lax.ppermute(f1, "cp", ahead)
    b2 = lax.ppermute(b1, "cp", back)
    f3 = lax.ppermute(f2, "cp", ahead)
    b3 = lax.ppermute(b2, "cp", back)
    f4 = lax.ppermute(f3, "cp", ahead)
    state = attend_first(table, counts, q_rot, unit, f1, b1, f2, b2, f3, b3)
    f4, state = tie((f4, state))
    own = jnp.concatenate([unit, f1, b1, f2, b2, f3, b3, f4], axis=0)

    mine, theirs = pick(routes, own)
    pages = mine + lax.ppermute(theirs, "cp", CORE_PAIRS)
    across = lax.ppermute(pages[1], ("cp", "tp"), MIRROR_PAIRS)
    pages, state = tie((pages, state))
    state = attend_middle(table, q_rot, state, f4)
    own, state = tie((own, state))
    other = lax.ppermute(own, "cp", CORE_PAIRS)
    across, state = tie((across, state))
    pages = lax.all_to_all(spread(pages, across), "tp", 0, 0, axis_index_groups=X_GROUPS)
    pages, attended = tie((pages, attend_rest(table, q_rot, state, other)))
    pool_keys, pool_values = place(routes, pages)
    return attended, pool_keys, pool_values


def solution(mesh):
    return jax.shard_map(
        shards,
        mesh=mesh,
        in_specs=(P("cp", "tp"), P("cp", "tp"), P("cp", "tp"), P(), P(), P(), P(), P()),
        out_specs=(P("cp", "tp"), P(("cp", "tp"), None, None), P(("cp", "tp"), None, None)),
        check_vma=False,
    )
```

```python
import functools
import math

import jax
import jax.numpy as jnp
import numpy as np
from jax import lax
from jax.experimental import pallas as pl
from jax.experimental.pallas import tpu as pltpu
from jax.sharding import PartitionSpec as P

KVH = 8
HD = 128
PAGE = 128
HALF = 64
ROWS = 128
N_CP = 64
N_Z = 4
N_Y = 8
N_TP = 8
N_X = 4
SRC = N_CP // 2
LANES = 128
RUNS = 2 * N_CP
BIG = 1e30

THETA = 500000.0
RATES = THETA ** (-np.arange(HALF) * 2.0 / HD)


def cos_sin(positions):
    angles = np.asarray(positions)[:, None] * np.concatenate([RATES, RATES])[None, :]
    return np.stack([np.cos(angles), np.sin(angles)]).astype(np.float32)


RUN_TABLE = cos_sin(np.arange(RUNS) * HALF)
STEP_TABLE = cos_sin(np.arange(HALF))


OFFSETS = (0, -1, 1, -2, 2, -3, 3, 4)
FIRST = 24
MIDDLE = SRC - FIRST
REST = SRC
BIG_GRANT = 24 * 2**20


def cp_index(z, y, core):
    return ((z % N_Z) * N_Y + y % N_Y) * 2 + core


def y_pairs(step):
    return [
        (cp_index(z, y, c), cp_index(z, y + step, c))
        for z in range(N_Z)
        for y in range(N_Y)
        for c in range(2)
    ]


Z_GROUPS = [[cp_index(z, y, c) for z in range(N_Z)] for y in range(N_Y) for c in range(2)]
X_GROUPS = [[hi * N_X + x for x in range(N_X)] for hi in range(2)]
CORE_PAIRS = [(i, i ^ 1) for i in range(N_CP)]
MIRROR_PAIRS = [
    (cp_index(z, y, c) * N_TP + tp, cp_index(N_Z - 1 - z, y, c) * N_TP + (tp ^ N_X))
    for z in range(N_Z)
    for y in range(N_Y)
    for c in range(2)
    for tp in range(N_TP)
]


def angles_of(run_table, step_table, first_run):
    low = lax.broadcasted_iota(jnp.int32, (HALF, HD), 1) < HALF
    cos, sin = [], []
    for run in (first_run, RUNS - 1 - first_run):
        run_cos, run_sin = run_table[0, pl.ds(run, 1), :], run_table[1, pl.ds(run, 1), :]
        cos.append(run_cos * step_table[0] - run_sin * step_table[1])
        part = run_sin * step_table[0] + run_cos * step_table[1]
        sin.append(jnp.where(low, -part, part))
    return jnp.concatenate(cos, axis=0), jnp.concatenate(sin, axis=0)


def turned(x, cos, sin):
    return x * cos + pltpu.roll(x, HALF, 1) * sin


SMEM = pl.BlockSpec(memory_space=pltpu.SMEM)
VMEM = pl.BlockSpec(memory_space=pltpu.VMEM)
ANY = pl.BlockSpec(memory_space=pl.ANY)


def coordinates():
    me = lax.axis_index("cp")
    return me, lax.div(me, 2 * N_Y), lax.rem(lax.div(me, 2), N_Y), lax.rem(me, 2)


def pack_kernel(positions, keys, values, run_table, step_table, out):
    first = lax.shift_right_logical(positions[lax.axis_index("cp") & 7, 0], 6)
    cos, sin = angles_of(run_table, step_table, first)
    k_rot = turned(keys[...].astype(jnp.float32), cos, sin).astype(jnp.bfloat16)
    v = values[...]
    for i in range(N_Z):
        out[i, 0] = k_rot
        out[i, 1] = v


def pack(positions, keys, values):
    def whole(*shape):
        return pl.BlockSpec(shape, lambda i: (0,) * len(shape))

    return pl.pallas_call(
        pack_kernel,
        grid=(1,),
        out_shape=jax.ShapeDtypeStruct((N_Z, 2, ROWS, HD), jnp.bfloat16),
        in_specs=[
            pl.BlockSpec(
                (8, ROWS),
                lambda i: (lax.div(lax.axis_index("cp"), 8), 0),
                memory_space=pltpu.SMEM,
            ),
            whole(ROWS, HD),
            whole(ROWS, HD),
            whole(2, RUNS, HD),
            whole(2, HALF, HD),
        ],
        out_specs=whole(N_Z, 2, ROWS, HD),
        cost_estimate=pl.CostEstimate(flops=1_000_000, bytes_accessed=400_000, transcendentals=0),
        name="pack",
    )(positions.reshape(N_CP, ROWS), keys, values, jnp.asarray(RUN_TABLE), jnp.asarray(STEP_TABLE))


def turn_kernel(positions, queries, run_table, step_table, q_rot, runs):
    for s in range(N_CP):
        runs[s] = lax.shift_right_logical(positions[s * ROWS], 6)
    my_run = runs[lax.axis_index("cp")]
    cos, sin = angles_of(run_table, step_table, my_run)
    for h in range(KVH):
        q = turned(queries[:, h * HD : (h + 1) * HD].astype(jnp.float32), cos, sin)
        q = q.astype(jnp.bfloat16)
        q_rot[0, h * HALF : (h + 1) * HALF, :] = q[:HALF]
        q_rot[1, h * HALF : (h + 1) * HALF, :] = q[HALF:]


def turn(positions, queries):
    return pl.pallas_call(
        turn_kernel,
        out_shape=(
            jax.ShapeDtypeStruct((2, KVH * HALF, HD), jnp.bfloat16),
            jax.ShapeDtypeStruct((N_CP,), jnp.int32),
        ),
        in_specs=[SMEM, VMEM, VMEM, VMEM],
        out_specs=(VMEM, SMEM),
        cost_estimate=pl.CostEstimate(flops=2_000_000, bytes_accessed=600_000, transcendentals=0),
        name="turn",
    )(positions, queries, jnp.asarray(RUN_TABLE), jnp.asarray(STEP_TABLE))


LIST_ROWS = ((0, 1), (2, 3), (4, 5))
MISC = 6
AT_COUNT, AT_RUN = 0, 8
BLOCKS = 7


def clip_valid(counts, run):
    return jnp.clip(counts[lax.shift_right_logical(run, 1)] - (run & 1) * HALF, 0, HALF)


def lists_kernel(runs, counts, owner_row, owner_col, owner_slot, table, routes):
    me, _, y_me, core = coordinates()
    my_run = runs[me]

    for part in range(3):
        side = part // 2
        start, stop = ((0, FIRST), (FIRST, SRC), (0, SRC))[part]
        n_low, n_high = jnp.int32(0), jnp.int32(0)
        low, high = LIST_ROWS[part]
        for b, at in enumerate(range(start, stop)):
            src_y = (y_me + OFFSETS[at // N_Z]) & (N_Y - 1)
            src_core = core if side == 0 else 1 - core
            run = runs[(at % N_Z) * 2 * N_Y + src_y * 2 + src_core]
            table[BLOCKS, run] = side * SRC + at
            first = b * 256 + clip_valid(counts, run)
            second = b * 256 + 128 + clip_valid(counts, RUNS - 1 - run)
            table[high, n_high] = first
            n_high = n_high + 1
            table[high, n_high] = second
            n_high = n_high + (run > my_run).astype(jnp.int32)
            table[low, n_low] = first
            n_low = n_low + (run < my_run).astype(jnp.int32)
        for r in range(16):
            table[low, n_low + r] = 0
            table[high, n_high + r] = 0
        table[MISC, AT_COUNT + low] = n_low
        table[MISC, AT_COUNT + high] = n_high
    table[MISC, AT_RUN] = my_run
    route_entries(table, counts, owner_row, owner_col, owner_slot, routes)


AT_PLACE, AT_PICK = 0, 8


def page_of(owner_row, head, me):
    page = jnp.int32(0)
    for p in range(N_CP):
        page = jnp.where(owner_row[head, p] == me, p, page)
    return page


def route_entries(lists, counts, owner_row, owner_col, owner_slot, table):
    me, z_me, _, _ = coordinates()
    tp = lax.axis_index("tp")
    for i in range(N_X):
        for d in range(2):
            head = i + ((tp & N_X) ^ (d * N_X))
            p = page_of(owner_row, head, me)
            mine = owner_col[head, p] == tp
            table[i * 2 + d] = jnp.where(mine, owner_slot[head, p], -1)

    for k in range(8):
        row = me if k < 4 else me ^ 1
        if k // 2 % 2 == 1:
            row = row + (N_Z - 1 - 2 * z_me) * 2 * N_Y
        if k % 2 == 0:
            page = page_of(owner_row, tp, row)
        run = page * 2 + k % 2
        second = run >= N_CP
        block = lists[BLOCKS, jnp.where(second, RUNS - 1 - run, run)]
        at = AT_PICK + 3 * k
        table[at] = block & (SRC - 1)
        table[at + 1] = second.astype(jnp.int32)
        table[at + 2] = jnp.where(block < SRC, clip_valid(counts, run), 0)


def lists(runs, counts, owner_row, owner_col, owner_slot):
    return pl.pallas_call(
        lists_kernel,
        out_shape=(
            jax.ShapeDtypeStruct((8, LANES), jnp.int32),
            jax.ShapeDtypeStruct((LANES,), jnp.int32),
        ),
        in_specs=[SMEM] * 5,
        out_specs=(SMEM, SMEM),
        cost_estimate=pl.CostEstimate(flops=2_000_000, bytes_accessed=300_000, transcendentals=0),
        name="lists",
    )(runs, counts, owner_row, owner_col, owner_slot)


COLS = KVH * HALF
SCALE = math.log2(math.e) / math.sqrt(HD)
dot = functools.partial(lax.dot_general, preferred_element_type=jnp.float32)


def fold(q, keys, vals, bias, allowed, state):
    top, total, acc = state
    s = dot(keys, q, (((1,), (1,)), ((), ()))) * SCALE
    s = s + jnp.concatenate([bias] * (COLS // HD), axis=1)
    if allowed is not None:
        s = jnp.where(allowed, s, -BIG)
    new_top = jnp.maximum(top, jnp.max(s, axis=0, keepdims=True))
    factor = jnp.exp2(top - new_top)
    w = jnp.exp2(s - new_top)
    total = total * factor + jnp.sum(w, axis=0, keepdims=True)
    acc = acc * factor + dot(vals, w.astype(jnp.bfloat16), (((0,), (0,)), ((), ())))
    return new_top, total, acc


def bias_of(valid):
    return jnp.where(lax.broadcasted_iota(jnp.int32, (HALF, HD), 0) < valid, 0.0, -BIG)


def fold_list(table, row, q, kv, state):
    def chunk(size, start, state):
        ks, vs, biases = [], [], []
        for r in range(size):
            code = table[row, start + r]
            b = lax.shift_right_logical(code, 8)
            rows = pl.ds(pl.multiple_of(lax.shift_right_logical(code & 128, 1), HALF), HALF)
            ks.append(kv[b, 0, rows, :])
            vs.append(kv[b, 1, rows, :])
            biases.append(bias_of(code & 127))
        return fold(
            q,
            jnp.concatenate(ks, axis=0),
            jnp.concatenate(vs, axis=0),
            jnp.concatenate(biases, axis=0),
            None,
            state,
        )

    count = table[MISC, AT_COUNT + row]
    wide = lax.shift_right_logical(count + 7, 4)
    state = lax.fori_loop(0, wide, lambda i, st: chunk(16, i * 16, st), state)
    narrow = (count > wide * 16).astype(jnp.int32)
    return lax.fori_loop(0, narrow, lambda i, st: chunk(8, wide * 16, st), state)


def copy_blocks(pieces, kv, sems):
    copies, at = [], 0
    for i, (piece, start, size) in enumerate(pieces):
        copies.append(
            pltpu.make_async_copy(
                piece.at[pl.ds(start, size)], kv.at[pl.ds(at, size)], sems.at[i]
            )
        )
        at += size
    for copy in copies:
        copy.start()
    for copy in copies:
        copy.wait()


def first_kernel(table, counts, q_rot, *refs):
    pieces, (tops, totals, accs, kv, sems) = refs[:-5], refs[-5:]
    copy_blocks([(piece, 0, N_Z) for piece in pieces], kv, sems)
    _, z_me, _, _ = coordinates()
    my_run = table[MISC, AT_RUN]
    key = lax.broadcasted_iota(jnp.int32, (HALF, COLS), 0)
    row = lax.broadcasted_iota(jnp.int32, (HALF, COLS), 1) & (HALF - 1)
    for part in range(2):
        q = q_rot[part]
        state = (
            jnp.full((1, COLS), -BIG, jnp.float32),
            jnp.zeros((1, COLS), jnp.float32),
            jnp.zeros((HD, COLS), jnp.float32),
        )
        run = my_run if part == 0 else RUNS - 1 - my_run
        page = lax.shift_right_logical(run, 1)
        valid = jnp.clip(counts[page] - (run & 1) * HALF, 0, HALF)
        rows = slice(part * HALF, (part + 1) * HALF)
        state = fold(q, kv[z_me, 0, rows], kv[z_me, 1, rows], bias_of(valid), key <= row, state)
        state = fold_list(table, LIST_ROWS[0][part], q, kv, state)
        tops[part], totals[part], accs[part] = state


STATE = (
    jax.ShapeDtypeStruct((2, 1, COLS), jnp.float32),
    jax.ShapeDtypeStruct((2, 1, COLS), jnp.float32),
    jax.ShapeDtypeStruct((2, HD, COLS), jnp.float32),
)


def attend_first(table, counts, q_rot, *pieces):
    return pl.pallas_call(
        first_kernel,
        out_shape=STATE,
        in_specs=[SMEM, SMEM, VMEM] + [ANY] * len(pieces),
        out_specs=(VMEM, VMEM, VMEM),
        scratch_shapes=[
            pltpu.VMEM((FIRST, 2, ROWS, HD), jnp.bfloat16),
            pltpu.SemaphoreType.DMA((len(pieces),)),
        ],
        compiler_params=pltpu.CompilerParams(vmem_limit_bytes=BIG_GRANT),
        cost_estimate=pl.CostEstimate(
            flops=6_000_000_000, bytes_accessed=3_000_000, transcendentals=2_000_000
        ),
        name="attend_first",
    )(table, counts, q_rot, *pieces)


def middle_kernel(table, q_rot, tops, totals, accs, b3, f4, new_tops, new_totals, new_accs, kv, sems):
    copy_blocks(((b3, 0, N_Z), (f4, 0, N_Z)), kv, sems)
    for part in range(2):
        state = tops[part], totals[part], accs[part]
        state = fold_list(table, LIST_ROWS[1][part], q_rot[part], kv, state)
        new_tops[part], new_totals[part], new_accs[part] = state


def attend_middle(table, q_rot, state, b3, f4):
    return pl.pallas_call(
        middle_kernel,
        out_shape=STATE,
        in_specs=[SMEM, VMEM, VMEM, VMEM, VMEM, ANY, ANY],
        out_specs=(VMEM, VMEM, VMEM),
        scratch_shapes=[
            pltpu.VMEM((MIDDLE, 2, ROWS, HD), jnp.bfloat16),
            pltpu.SemaphoreType.DMA((2,)),
        ],
        compiler_params=pltpu.CompilerParams(vmem_limit_bytes=BIG_GRANT),
        cost_estimate=pl.CostEstimate(
            flops=2_000_000_000, bytes_accessed=2_000_000, transcendentals=1_000_000
        ),
        name="attend_middle",
    )(table, q_rot, *state, b3, f4)


def rest_kernel(table, q_rot, tops, totals, accs, other, out, kv, sem):
    copy = pltpu.make_async_copy(other, kv, sem)
    copy.start()
    copy.wait()
    for part in range(2):
        state = tops[part], totals[part], accs[part]
        _, total, acc = fold_list(table, LIST_ROWS[2][part], q_rot[part], kv, state)
        res = jnp.transpose(acc / total).astype(jnp.bfloat16)
        for h in range(KVH):
            out[part * HALF : (part + 1) * HALF, h * HD : (h + 1) * HD] = res[
                h * HALF : (h + 1) * HALF
            ]


def attend_rest(table, q_rot, state, other):
    return pl.pallas_call(
        rest_kernel,
        out_shape=jax.ShapeDtypeStruct((ROWS, KVH * HD), jnp.bfloat16),
        in_specs=[SMEM, VMEM, VMEM, VMEM, VMEM, ANY],
        out_specs=VMEM,
        scratch_shapes=[
            pltpu.VMEM((REST, 2, ROWS, HD), jnp.bfloat16),
            pltpu.SemaphoreType.DMA,
        ],
        compiler_params=pltpu.CompilerParams(vmem_limit_bytes=BIG_GRANT),
        cost_estimate=pl.CostEstimate(
            flops=8_000_000_000, bytes_accessed=4_000_000, transcendentals=2_000_000
        ),
        name="attend_rest",
    )(table, q_rot, *state, other)


def pick_kernel(table, own, mine, theirs, held, sems):
    copies = []
    for k in range(8):
        index, second = table[AT_PICK + 3 * k], table[AT_PICK + 3 * k + 1]
        rows = pl.ds(pl.multiple_of(second * HALF, HALF), HALF)
        copies.append(pltpu.make_async_copy(own.at[index, :, rows], held.at[k], sems.at[k]))
        copies[-1].start()
    row = lax.broadcasted_iota(jnp.int32, (HALF, HD), 0)
    for k in range(8):
        copies[k].wait()
        keep = row < table[AT_PICK + 3 * k + 2]
        out = mine if k < 4 else theirs
        rows = slice(k % 2 * HALF, (k % 2 + 1) * HALF)
        for i in range(2):
            out[k // 2 % 2, i, rows, :] = jnp.where(
                keep, held[k, i].astype(jnp.float32), 0.0
            ).astype(jnp.bfloat16)


def pick(table, own):
    pages = jax.ShapeDtypeStruct((2, 2, PAGE, HD), jnp.bfloat16)
    return pl.pallas_call(
        pick_kernel,
        out_shape=(pages, pages),
        in_specs=[SMEM, ANY],
        out_specs=(VMEM, VMEM),
        scratch_shapes=[
            pltpu.VMEM((8, 2, HALF, HD), jnp.bfloat16),
            pltpu.SemaphoreType.DMA((8,)),
        ],
        compiler_params=pltpu.CompilerParams(vmem_limit_bytes=BIG_GRANT),
        cost_estimate=pl.CostEstimate(flops=100_000, bytes_accessed=300_000, transcendentals=0),
        name="pick",
    )(table, own)


def spread_kernel(mine, across, out):
    for i in range(N_X):
        out[i, 0] = mine[0]
        out[i, 1] = across[...]


def spread(mine, across):
    return pl.pallas_call(
        spread_kernel,
        grid=(1,),
        out_shape=jax.ShapeDtypeStruct((N_X, 2, 2, PAGE, HD), jnp.bfloat16),
        in_specs=[
            pl.BlockSpec((1, 2, PAGE, HD), lambda i: (0, 0, 0, 0)),
            pl.BlockSpec((2, PAGE, HD), lambda i: (0, 0, 0)),
        ],
        out_specs=pl.BlockSpec((N_X, 2, 2, PAGE, HD), lambda i: (0, 0, 0, 0, 0)),
        compiler_params=pltpu.CompilerParams(vmem_limit_bytes=BIG_GRANT),
        cost_estimate=pl.CostEstimate(
            flops=100_000_000_000, bytes_accessed=700_000, transcendentals=0
        ),
        name="spread",
    )(mine, across)


def place_kernel(table, pages, pool_k, pool_v, sems):
    for slot in range(2):
        empty = True
        for i in range(N_X):
            for hi in range(2):
                hit = table[i * 2 + hi] == slot
                empty = jnp.logical_and(empty, jnp.logical_not(hit))

                @pl.when(hit)
                def _(i=i, hi=hi, slot=slot):
                    pltpu.make_async_copy(pages.at[i, hi, 0], pool_k.at[slot], sems.at[slot, 0]).start()
                    pltpu.make_async_copy(pages.at[i, hi, 1], pool_v.at[slot], sems.at[slot, 1]).start()

        @pl.when(empty)
        def _(slot=slot):
            pool_k[slot] = jnp.zeros((PAGE, HD), jnp.bfloat16)
            pool_v[slot] = jnp.zeros((PAGE, HD), jnp.bfloat16)

        @pl.when(jnp.logical_not(empty))
        def _(slot=slot):
            pltpu.make_async_copy(pages.at[0, 0, 0], pool_k.at[slot], sems.at[slot, 0]).wait()
            pltpu.make_async_copy(pages.at[0, 0, 1], pool_v.at[slot], sems.at[slot, 1]).wait()


def place(table, pages):
    shape = jax.ShapeDtypeStruct((2, PAGE, HD), jnp.bfloat16)
    return pl.pallas_call(
        place_kernel,
        out_shape=(shape, shape),
        in_specs=[SMEM, ANY],
        out_specs=(VMEM, VMEM),
        scratch_shapes=[pltpu.SemaphoreType.DMA((2, 2))],
        compiler_params=pltpu.CompilerParams(vmem_limit_bytes=BIG_GRANT),
        cost_estimate=pl.CostEstimate(flops=100_000, bytes_accessed=800_000, transcendentals=0),
        name="place",
    )(table, pages)


def shards(queries, keys, values, positions, counts, owner_row, owner_col, owner_slot):
    tie = lax.optimization_barrier
    packed, later_positions = tie((pack(positions, keys, values), positions))
    unit = lax.all_to_all(packed, "cp", 0, 0, axis_index_groups=Z_GROUPS)
    q_rot, runs = turn(later_positions, queries)
    table, routes = lists(runs, counts, owner_row, owner_col, owner_slot)
    unit, q_rot, table, routes = tie((unit, q_rot, table, routes))

    ahead, back = y_pairs(1), y_pairs(-1)
    f1 = lax.ppermute(unit, "cp", ahead)
    b1 = lax.ppermute(unit, "cp", back)
    f2 = lax.ppermute(f1, "cp", ahead)
    b2 = lax.ppermute(b1, "cp", back)
    f3 = lax.ppermute(f2, "cp", ahead)
    b3 = lax.ppermute(b2, "cp", back)
    f4 = lax.ppermute(f3, "cp", ahead)
    state = attend_first(table, counts, q_rot, unit, f1, b1, f2, b2, f3)
    f4, state = tie((f4, state))
    own = jnp.concatenate([unit, f1, b1, f2, b2, f3, b3, f4], axis=0)

    mine, theirs = pick(routes, own)
    pages = mine + lax.ppermute(theirs, "cp", CORE_PAIRS)
    across = lax.ppermute(pages[1], ("cp", "tp"), MIRROR_PAIRS)
    pages, state = tie((pages, state))
    state = attend_middle(table, q_rot, state, b3, f4)
    own, state = tie((own, state))
    other = lax.ppermute(own, "cp", CORE_PAIRS)
    across, state = tie((across, state))
    pages = lax.all_to_all(spread(pages, across), "tp", 0, 0, axis_index_groups=X_GROUPS)
    pages, attended = tie((pages, attend_rest(table, q_rot, state, other)))
    pool_keys, pool_values = place(routes, pages)
    return attended, pool_keys, pool_values


def solution(mesh):
    return jax.shard_map(
        shards,
        mesh=mesh,
        in_specs=(P("cp", "tp"), P("cp", "tp"), P("cp", "tp"), P(), P(), P(), P(), P()),
        out_specs=(P("cp", "tp"), P(("cp", "tp"), None, None), P(("cp", "tp"), None, None)),
        check_vma=False,
    )
```
